256 devices in a mesh: row: 16 (over x, z_hi, core), col: 16 (over y, z_lo).
Axes of the slice: x: 4, y: 4, z: 8 (z_hi: 2, z_lo: 4; z = z_hi * 4 + z_lo), core: 2. Of those that a mesh axis runs over, the one named last changes fastest.
Arguments:
- surface: bfloat16 [2048, 118784], P(None, ('row', 'col')), may hold values from -24 to 24
- eigvec: bfloat16 [118784, 2048], P('row', 'col'), may hold values from -0.015625 to 0.015625
- eig_energy: float32 [2048], replicated, may hold values from 1 to 10
- energies: float32 [8], replicated, may hold values from -1 to 0.5
Outputs:
- amplitudes: float32 [2048, 2048], P('row', 'col')
- rmatrix: float32 [8, 2048, 2048], P(None, 'row', 'col')
The draws below stay inside these ranges and needn't reach their ends.
All inputs are finite; a program needn't handle non-finite values.
Results may differ from the reference program's by a relative error of at most 0.0003.
Values may be sent and summed in bfloat16 or wider, within the bound.
A program may use at most 64 MiB of HBM per device.

```python
import math
import jax
import jax.numpy as jnp
from jax import lax

C = 2048
K = 2048
R_DEV = 464
NE = 8
R = 118784
N_ROW = 16
N_COL = 16


def raised(result, stream_key, source, target, parts, factor):
    def block_of(position):
        return (jnp.arange(result.shape[position]) // (result.shape[position] // parts)).reshape((-1,) + (1,) * (result.ndim - 1 - position))

    first = jax.random.permutation(stream_key, parts)[block_of(target)]
    other_side = (block_of(target) + parts // 2) % parts
    return jnp.where((block_of(source) == first) | (block_of(source) == other_side), factor * result, result)


def block_levels(own_key, dims, pieces, low, high):
    level = 1.0
    for axis_at, shards_of in pieces:
        steps = jax.random.uniform(jax.random.fold_in(jax.random.fold_in(own_key, 6), axis_at), (shards_of,), jnp.float32, low / len(pieces), high / len(pieces))
        level = level * jnp.repeat(jnp.exp(steps), dims[axis_at] // shards_of).reshape((-1,) + (1,) * (len(dims) - 1 - axis_at))
    return level


def scatter_about(rng, dims, spread, bound, pieces=(), held_as=jnp.bfloat16):
    drawn = jax.random.normal(rng, dims, jnp.float32) * spread
    if len(pieces) > 0:
        drawn = block_levels(rng, dims, pieces, -0.22, 0.18) * drawn
    return jnp.clip(drawn, min=-bound, max=bound).astype(held_as)


def gaussian_with(stream_key, dims, scale, limit, cuts, heavy, kind=jnp.bfloat16):
    drawn = scale * jax.random.normal(stream_key, dims, jnp.float32)
    if cuts:
        drawn = drawn * block_levels(stream_key, dims, cuts, -0.22, 0.18)
    return jnp.clip(raised(drawn, jax.random.fold_in(stream_key, 3), *heavy), -limit, limit).astype(kind)


def setup_inputs(seed: int = 0) -> dict:
    seeds = jax.random.split(jax.random.key(seed), 5)
    return {
        "surface": gaussian_with(seeds[0], (C, R), 1.0, 24.0, ((1, 256),), (1, 0, 256, 6.0)),
        "eigvec": scatter_about(seeds[1], (R, K), R ** -0.5, 0.015625, ((0, 16), (1, 16))),
        "eig_energy": jnp.clip(jnp.exp(jax.random.uniform(seeds[2], (K,), jnp.float32, math.log(1.0), math.log(10.0))), 1.0, 10.0),
        "energies": jnp.clip(jax.random.uniform(seeds[3], (NE,), jnp.float32, -1.0, 0.5), -1.0, 0.5),
    }


def reference(surface, eigvec, eig_energy, energies):
    block = R_DEV * N_COL
    width = eig_energy.shape[0]

    def accumulate(total, index):
        start = (index * block).astype(jnp.int32)
        left = lax.dynamic_slice_in_dim(surface, start, block, 1)
        right = lax.dynamic_slice_in_dim(eigvec, start, block, 0)
        return (total + jnp.dot(left, right, preferred_element_type=jnp.float32), None)
    amplitudes, unused = lax.scan(accumulate, jnp.zeros((surface.shape[0], width), jnp.float32), jnp.arange(N_ROW, dtype=jnp.int32))
    poles = 1.0 / (eig_energy[None, :] - energies[:, None])
    factor = 1.0 / math.sqrt(width)

    def one_energy(weights):
        scaled = amplitudes * weights[None, :]
        product = lax.dot_general(scaled, amplitudes, (((1,), (1,)), ((), ())), precision=lax.Precision.HIGHEST, preferred_element_type=jnp.float32)
        return product * factor
    rmatrix = lax.map(one_energy, poles)
    return (amplitudes, rmatrix)
```

```python
import functools
import math

import jax
import jax.numpy as jnp
from jax import lax
from jax.experimental import pallas as pl
from jax.experimental.pallas import tpu as pltpu
from jax.sharding import PartitionSpec as P

MESH = pl.DeviceIdType.MESH
XR = (0, 40)
YR = (40, 48)
ZR = (88, 40)
XY = XR[1] + YR[1]


def rows(part):
    return pl.ds(part[0], part[1])


def copy_to(device, src, dst, send, recv):
    return pltpu.make_async_remote_copy(
        src_ref=src, dst_ref=dst, send_sem=send, recv_sem=recv, device_id=device, device_id_type=MESH
    )


def add_into(dst, *srcs):
    shape = dst.shape
    if len(shape) == 2:
        total = dst[...]
        for s in srcs:
            total = total + s[...]
        dst[...] = total
        return
    lead = shape[:-2]
    count = math.prod(lead)

    def body(i, carry):
        at = (i,) if len(lead) == 1 else (i // lead[1], i % lead[1])
        total = dst[at]
        for s in srcs:
            total = total + s[at]
        dst[at] = total
        return carry

    lax.fori_loop(0, count, body, 0)


class Ring4:
    def __init__(self, at, plus, minus, chunk, far, near, send, recv):
        self.at, self.chunk, self.near = at, chunk, near
        up, down, across = (at + 1) % 4, (at + 3) % 4, (at + 2) % 4
        self.up, self.down, self.far = up, down, far
        c = functools.partial
        self.p1 = copy_to(plus, chunk(across, 0), far.at[0], send.at[0], recv.at[0])
        self.m1 = copy_to(minus, chunk(across, 1), far.at[1], send.at[1], recv.at[1])
        self.p2 = copy_to(plus, chunk(up, 1), near.at[0, 1], send.at[2], recv.at[2])
        self.m2 = copy_to(minus, chunk(down, 0), near.at[1, 0], send.at[3], recv.at[3])
        self.p3 = copy_to(plus, chunk(up, 0), near.at[0, 0], send.at[4], recv.at[4])
        self.m3 = copy_to(minus, chunk(down, 1), near.at[1, 1], send.at[5], recv.at[5])

    def start(self):
        for c in (self.p1, self.m1, self.p2, self.m2):
            c.start()

    def middle(self):
        self.p1.wait_recv()
        add_into(self.chunk(self.up, 0), self.far.at[0])
        self.p3.start()
        self.m1.wait_recv()
        add_into(self.chunk(self.down, 1), self.far.at[1])
        self.m3.start()

    def finish(self):
        for c in (self.p2, self.m2, self.p3, self.m3):
            c.wait_recv()
        for h in range(2):
            add_into(self.chunk(self.at, h), self.near.at[0, h], self.near.at[1, h])

    def close(self):
        for c in (self.p1, self.m1, self.p2, self.m2, self.p3, self.m3):
            c.wait_send()


class Ring8:
    def __init__(self, at, plus, minus, chunk, slots, send, recv):
        self.at, self.chunk, self.slots = at, chunk, slots
        self.copies, self.held = [], []
        for s in range(7):
            k = 4 - (s + 1) // 2
            h = 0 if s % 2 == 0 else 1
            pair, held = [], []
            for way, device in ((0, plus), (1, minus)):
                i = (at + k) % 8 if way == 0 else (at + 8 - k) % 8
                half = h if way == 0 else 1 - h
                view = chunk(i, half)
                held.append(view)
                pair.append(copy_to(device, view, slots.at[way, s], send.at[way, s], recv.at[way, s]))
            self.copies.append(pair)
            self.held.append(held)

    def start(self):
        for s in range(2):
            for c in self.copies[s]:
                c.start()

    def step(self, s):
        for way in range(2):
            self.copies[s - 2][way].wait_recv()
            add_into(self.held[s][way], self.slots.at[way, s - 2])
            self.copies[s][way].start()

    def finish(self):
        for s in (5, 6):
            for way in range(2):
                self.copies[s][way].wait_recv()
        add_into(self.chunk(self.at, 0), self.slots.at[0, 6], self.slots.at[1, 5])
        add_into(self.chunk(self.at, 1), self.slots.at[0, 5], self.slots.at[1, 6])

    def close(self):
        for pair in self.copies:
            for c in pair:
                c.wait_send()


def kernel(
    surf, eig, levels, energies, amp_out, r_out,
    s_buf, v_buf, part, xfar, xnear, yfar, ynear, zslot, x2far, x2near, y2far, y2near, w2far, w2near,
    z3, y3, ar, ac, pole,
    loc_sem, s_sem, a_send, a_recv, f_send, f_recv,
    x_sem, y_sem, z_sem, x2_sem, y2_sem, w2_sem, z3_sem, y3_sem, t1_sem, t1y_sem, t2_send, t2_recv, t3_sem,
):
    row, col = lax.axis_index("row"), lax.axis_index("col")
    x, zhi, core = row // 4, (row // 2) % 2, row % 2
    y, zlo = col // 4, col % 4
    z = zhi * 4 + zlo
    other = (row + 1 - 2 * core, col)

    def at_x(i):
        return ((i % 4) * 4 + zhi * 2 + core, col)

    def at_y(i):
        return (row, (i % 4) * 4 + zlo)

    def at_z(i):
        i = i % 8
        return (x * 4 + (i // 4) * 2 + core, y * 4 + i % 4)

    load_s = pltpu.make_async_copy(surf.at[:, core], s_buf.at[0], loc_sem.at[0])
    load_s.start()
    load_v = pltpu.make_async_copy(eig.at[col], v_buf.at[0, 0], loc_sem.at[1])
    load_v.start()

    barrier = pltpu.get_barrier_semaphore()

    def greet(device):
        pl.semaphore_signal(barrier, inc=1, device_id=device, device_id_type=MESH)

    def greet_col(j, carry):
        greet((row, ((y + j // 4) % 4) * 4 + (zlo + j % 4) % 4))
        return carry

    lax.fori_loop(1, 16, greet_col, 0)
    greet(other)
    greet(at_x(x + 1))
    greet(at_x(x + 3))

    def greet_z(j, carry):
        greet((x * 4 + (1 - zhi) * 2 + core, y * 4 + j))
        return carry

    lax.fori_loop(0, 4, greet_z, 0)

    def greet_t2(j, carry):
        source = 2 * j + core

        @pl.when(jnp.logical_or(row != col, source != col))
        def _():
            greet((col, source))

        return carry

    lax.fori_loop(0, 8, greet_t2, 0)
    diagonal = row == col
    pl.semaphore_wait(barrier, jnp.where(diagonal, 29, 30))

    def a2a(j):
        dest = ((y + j % 4) % 4) * 4 + (zlo + j // 4) % 4
        return copy_to((row, dest), eig.at[dest], v_buf.at[0, j], a_send.at[j], a_recv.at[j])

    def order(i):
        return jnp.where(i == 0, 0, (i + 2) % 15 + 1)

    def send_a2a(i, carry):
        a2a(order(i)).start()
        return carry

    lax.fori_loop(1, 16, send_a2a, 0)
    give_s = copy_to(other, surf.at[:, 1 - core], s_buf.at[1], s_sem.at[0], s_sem.at[1])
    give_s.start()

    pole[...] = (1.0 / math.sqrt(2048.0)) / (levels[...] - energies[...])

    def forward(j):
        return copy_to(other, v_buf.at[0, j], v_buf.at[1, j], f_send.at[j], f_recv.at[j])

    load_v.wait()
    forward(0).start()
    load_s.wait()
    give_s.wait_recv()

    def multiply(j):
        forward(j).wait_recv()
        ys, zs = (y + 4 - j % 4) % 4, (zlo + 4 - j // 4) % 4
        width = s_buf.shape[-1]
        got = jnp.dot(s_buf[0].reshape(1024, width), v_buf[0, j], preferred_element_type=jnp.float32)
        got += jnp.dot(s_buf[1].reshape(1024, width), v_buf[1, j], preferred_element_type=jnp.float32)
        got = got.reshape(4, 2, 128, 128)
        for xi in range(4):
            for zh in range(2):
                part[xi, ys, zh * 4 + zs] = got[xi, zh]

    def take(i, carry):
        j = order(i)

        @pl.when(i < 16)
        def _():
            a2a(j).wait_recv()
            forward(j).start()

        multiply(order(i - 1))
        return carry

    lax.fori_loop(1, 17, take, 0)

    ring_x = Ring4(x, at_x(x + 1), at_x(x + 3), lambda i, h: part.at[i, :, pl.ds(4 * h, 4), rows(XR)],
                   xfar, xnear, x_sem.at[0], x_sem.at[1])
    ring_y = Ring4(y, at_y(y + 1), at_y(y + 3), lambda i, h: part.at[:, i, pl.ds(4 * h, 4), rows(YR)],
                   yfar, ynear, y_sem.at[0], y_sem.at[1])
    ring_z = Ring8(z, at_z(z + 1), at_z(z + 7), lambda i, h: part.at[pl.ds(2 * h, 2), :, i, rows(ZR)],
                   zslot, z_sem.at[0], z_sem.at[1])
    ring_xy = Ring4(y, at_y(y + 1), at_y(y + 3), lambda i, h: part.at[x, i, pl.ds(4 * h, 4), rows(XR)],
                    x2far, x2near, x2_sem.at[0], x2_sem.at[1])
    ring_yx = Ring4(x, at_x(x + 1), at_x(x + 3), lambda i, h: part.at[i, y, pl.ds(4 * h, 4), rows(YR)],
                    y2far, y2near, y2_sem.at[0], y2_sem.at[1])
    ring_zx = Ring4(x, at_x(x + 1), at_x(x + 3), lambda i, h: part.at[i, pl.ds(2 * h, 2), z, rows(ZR)],
                    w2far, w2near, w2_sem.at[0], w2_sem.at[1])
    ring_z.start()
    ring_x.start()
    ring_y.start()
    ring_z.step(2)
    ring_z.step(3)
    ring_x.middle()
    ring_y.middle()
    ring_z.step(4)
    ring_z.step(5)
    ring_z.step(6)
    ring_x.finish()
    ring_xy.start()
    ring_z.finish()
    ring_zx.start()
    ring_y.finish()
    ring_yx.start()
    ring_xy.middle()
    ring_zx.middle()
    ring_yx.middle()
    ring_xy.finish()
    ring_zx.finish()
    ring_yx.finish()
    rest_z = []
    for k in range(1, 8):
        rest_z.append(copy_to(at_z(z + k), part.at[x, y, (z + k) % 8, pl.ds(0, XY)], z3.at[k - 1],
                              z3_sem.at[0, k - 1], z3_sem.at[1, k - 1]))
        rest_z[-1].start()
    rest_y = []
    for k in range(1, 4):
        rest_y.append(copy_to(at_y(y + k), part.at[x, (y + k) % 4, z, rows(ZR)], y3.at[k - 1],
                              y3_sem.at[0, k - 1], y3_sem.at[1, k - 1]))
        rest_y[-1].start()
    total = part[x, y, z, ZR[0]:]
    for k, c in enumerate(rest_y):
        c.wait_recv()
        total = total + y3[k]
    ar[col, ZR[0]:] = total
    total = part[x, y, z, :XY]
    for k, c in enumerate(rest_z):
        c.wait_recv()
        total = total + z3[k]
    ar[col, :XY] = total
    amp_out[...] = ar[col]

    def t1(k):
        return copy_to((row, y * 4 + (zlo + k) % 4), ar.at[col], ar.at[col], t1_sem.at[0, k], t1_sem.at[1, k])

    def t1_from(k):
        there = y * 4 + (zlo + 4 - k) % 4
        return copy_to((row, there), ar.at[there], ar.at[there], t1_sem.at[0, k], t1_sem.at[1, k])

    def t1y(j, k):
        held = y * 4 + (zlo + 4 - j) % 4
        return copy_to(at_y(y + k), ar.at[held], ar.at[held], t1y_sem.at[0, j, k], t1y_sem.at[1, j, k])

    def t1y_from(j, k):
        there = ((y + 4 - k) % 4) * 4 + (zlo + 4 - j) % 4
        return copy_to(at_y(y + k), ar.at[there], ar.at[there], t1y_sem.at[0, j, k], t1y_sem.at[1, j, k])

    half = zlo % 2

    def t2(i):
        device = (((x + i // 2) % 4) * 4 + ((zhi + i % 2) % 2) * 2 + half, row)
        return copy_to(device, ar.at[col], ac.at[col], t2_send.at[i], t2_recv.at[col // 2])

    stay = pltpu.make_async_copy(ar.at[col], ac.at[col], t2_recv.at[col // 2])
    for k in range(1, 4):
        t1(k).start()

    @pl.when(diagonal)
    def _():
        stay.start()

    @pl.when(jnp.logical_not(diagonal))
    def _():
        t2(0).start()

    for k in range(1, 4):
        t1y(0, k).start()
    for i in range(1, 8):
        t2(i).start()
    for j in range(1, 4):
        t1_from(j).wait_recv()
        for k in range(1, 4):
            t1y(j, k).start()

    def t3(s):
        return copy_to(other, ac.at[s], ac.at[s], t3_sem.at[0, s], t3_sem.at[1, s])

    def pass_on(j, carry):
        s = 2 * j + core
        copy_to(other, ac.at[s], ac.at[s], t2_send.at[0], t2_recv.at[j]).wait_recv()
        t3(s).start()
        return carry

    lax.fori_loop(0, 8, pass_on, 0)
    for j in range(4):
        for k in range(1, 4):
            t1y_from(j, k).wait_recv()

    def await_other(j, carry):
        t3(2 * j + 1 - core).wait_recv()
        return carry

    lax.fori_loop(0, 8, await_other, 0)

    r_out[...] = jnp.zeros_like(r_out)

    def pair(i, carry):
        a = jnp.concatenate([ar[2 * i], ar[2 * i + 1]], axis=1)
        b = jnp.concatenate([ac[2 * i], ac[2 * i + 1]], axis=1)
        b_hi = b.astype(jnp.bfloat16)
        b_lo = (b - b_hi.astype(jnp.float32)).astype(jnp.bfloat16)
        both = jnp.concatenate([b_hi, b_lo], axis=0)
        p = pole[:, pl.ds(pl.multiple_of(256 * i, 256), 256)]
        his, los = [], []
        for e in range(8):
            scaled = a * p[e:e + 1]
            hi = scaled.astype(jnp.bfloat16)
            his.append(hi)
            los.append((scaled - hi.astype(jnp.float32)).astype(jnp.bfloat16))
        hi = jnp.concatenate(his, axis=0)
        lo = jnp.concatenate(los, axis=0)
        contract = (((1,), (1,)), ((), ()))
        one = lax.dot_general(hi, both, contract, preferred_element_type=jnp.float32)
        two = lax.dot_general(lo, b_hi, contract, preferred_element_type=jnp.float32)
        r_out[...] += (one[:, :128] + (one[:, 128:] + two)).reshape(8, 128, 128)
        return carry

    lax.fori_loop(0, 8, pair, 0)

    def close_a2a(j, carry):
        a2a(j).wait_send()
        return carry

    lax.fori_loop(1, 16, close_a2a, 0)

    def close_forward(j, carry):
        forward(j).wait_send()
        return carry

    lax.fori_loop(0, 16, close_forward, 0)
    give_s.wait_send()
    for ring in (ring_x, ring_y, ring_z, ring_xy, ring_yx, ring_zx):
        ring.close()
    for c in rest_z + rest_y:
        c.wait_send()
    for k in range(1, 4):
        t1(k).wait_send()
        for j in range(4):
            t1y(j, k).wait_send()

    @pl.when(jnp.logical_not(diagonal))
    def _():
        t2(0).wait_send()

    for i in range(1, 8):
        t2(i).wait_send()

    def close_t3(j, carry):
        t3(2 * j + core).wait_send()
        return carry

    lax.fori_loop(0, 8, close_t3, 0)


def local(surface, eigvec, eig_energy, energies):
    width = surface.shape[1]
    f32, bf16 = jnp.float32, jnp.bfloat16
    dma = pltpu.SemaphoreType.DMA
    nx, ny, nz = XR[1], YR[1], ZR[1]
    vmem = pl.BlockSpec(memory_space=pltpu.VMEM)
    return pl.pallas_call(
        kernel,
        out_shape=(jax.ShapeDtypeStruct((128, 128), f32), jax.ShapeDtypeStruct((8, 128, 128), f32)),
        in_specs=[pl.BlockSpec(memory_space=pl.ANY)] * 2 + [vmem] * 2,
        out_specs=(vmem, vmem),
        scratch_shapes=[
            pltpu.VMEM((2, 8, 128, width), bf16),
            pltpu.VMEM((2, 16, width, 128), bf16),
            pltpu.VMEM((4, 4, 8, 128, 128), f32),
            pltpu.VMEM((2, 4, 4, nx, 128), f32),
            pltpu.VMEM((2, 2, 4, 4, nx, 128), f32),
            pltpu.VMEM((2, 4, 4, ny, 128), f32),
            pltpu.VMEM((2, 2, 4, 4, ny, 128), f32),
            pltpu.VMEM((2, 7, 2, 4, nz, 128), f32),
            pltpu.VMEM((2, 4, nx, 128), f32),
            pltpu.VMEM((2, 2, 4, nx, 128), f32),
            pltpu.VMEM((2, 4, ny, 128), f32),
            pltpu.VMEM((2, 2, 4, ny, 128), f32),
            pltpu.VMEM((2, 2, nz, 128), f32),
            pltpu.VMEM((2, 2, 2, nz, 128), f32),
            pltpu.VMEM((7, XY, 128), f32),
            pltpu.VMEM((3, nz, 128), f32),
            pltpu.VMEM((16, 128, 128), f32),
            pltpu.VMEM((16, 128, 128), f32),
            pltpu.VMEM((8, 2048), f32),
            dma((2,)), dma((2,)), dma((16,)), dma((16,)), dma((16,)), dma((16,)),
            dma((2, 6)), dma((2, 6)), dma((2, 2, 7)), dma((2, 6)), dma((2, 6)), dma((2, 6)),
            dma((2, 7)), dma((2, 3)), dma((2, 4)), dma((2, 4, 4)), dma((8,)), dma((8,)), dma((2, 16)),
        ],
        compiler_params=pltpu.CompilerParams(
            collective_id=0, has_side_effects=True, vmem_limit_bytes=48 * 1024 * 1024
        ),
    )(
        surface.reshape(8, 2, 128, width),
        eigvec.reshape(16, width, 128),
        eig_energy.reshape(1, -1),
        energies.reshape(-1, 1),
    )


def solution(mesh):
    in_specs = (P(None, ("row", "col")), P("row", "col"), P(), P())
    out_specs = (P("row", "col"), P(None, "row", "col"))
    return jax.shard_map(local, mesh=mesh, in_specs=in_specs, out_specs=out_specs, check_vma=False)
```

```python
import functools
import math

import jax
import jax.numpy as jnp
from jax import lax
from jax.experimental import pallas as pl
from jax.experimental.pallas import tpu as pltpu
from jax.sharding import PartitionSpec as P

MESH = pl.DeviceIdType.MESH
GROUPS = ((32, 24, 8), (32, 16, 16))


def copy_to(device, src, dst, send, recv):
    return pltpu.make_async_remote_copy(
        src_ref=src, dst_ref=dst, send_sem=send, recv_sem=recv, device_id=device, device_id_type=MESH
    )


def add_into(dst, *srcs):
    shape = dst.shape
    if len(shape) == 2:
        total = dst[...]
        for s in srcs:
            total = total + s[...]
        dst[...] = total
        return
    lead = shape[:-2]
    count = math.prod(lead)

    def body(i, carry):
        at = (i,) if len(lead) == 1 else (i // lead[1], i % lead[1])
        total = dst[at]
        for s in srcs:
            total = total + s[at]
        dst[at] = total
        return carry

    lax.fori_loop(0, count, body, 0)


class Ring4:
    def __init__(self, at, plus, minus, chunk, far, near, send, recv):
        self.at, self.chunk, self.near = at, chunk, near
        up, down, across = (at + 1) % 4, (at + 3) % 4, (at + 2) % 4
        self.up, self.down, self.far = up, down, far
        c = functools.partial
        self.p1 = copy_to(plus, chunk(across, 0), far.at[0], send.at[0], recv.at[0])
        self.m1 = copy_to(minus, chunk(across, 1), far.at[1], send.at[1], recv.at[1])
        self.p2 = copy_to(plus, chunk(up, 1), near.at[0, 1], send.at[2], recv.at[2])
        self.m2 = copy_to(minus, chunk(down, 0), near.at[1, 0], send.at[3], recv.at[3])
        self.p3 = copy_to(plus, chunk(up, 0), near.at[0, 0], send.at[4], recv.at[4])
        self.m3 = copy_to(minus, chunk(down, 1), near.at[1, 1], send.at[5], recv.at[5])

    def start(self):
        for c in (self.p1, self.m1, self.p2, self.m2):
            c.start()

    def middle(self):
        self.p1.wait_recv()
        add_into(self.chunk(self.up, 0), self.far.at[0])
        self.p3.start()
        self.m1.wait_recv()
        add_into(self.chunk(self.down, 1), self.far.at[1])
        self.m3.start()

    def finish(self):
        for c in (self.p2, self.m2, self.p3, self.m3):
            c.wait_recv()
        for h in range(2):
            add_into(self.chunk(self.at, h), self.near.at[0, h], self.near.at[1, h])

    def close(self):
        for c in (self.p1, self.m1, self.p2, self.m2, self.p3, self.m3):
            c.wait_send()


class Ring8:
    def __init__(self, at, plus, minus, chunk, slots, send, recv):
        self.at, self.chunk, self.slots = at, chunk, slots
        self.copies, self.held = [], []
        for s in range(7):
            k = 4 - (s + 1) // 2
            h = 0 if s % 2 == 0 else 1
            pair, held = [], []
            for way, device in ((0, plus), (1, minus)):
                i = (at + k) % 8 if way == 0 else (at + 8 - k) % 8
                half = h if way == 0 else 1 - h
                view = chunk(i, half)
                held.append(view)
                pair.append(copy_to(device, view, slots.at[way, s], send.at[way, s], recv.at[way, s]))
            self.copies.append(pair)
            self.held.append(held)

    def start(self):
        for s in range(2):
            for c in self.copies[s]:
                c.start()

    def step(self, s):
        for way in range(2):
            self.copies[s - 2][way].wait_recv()
            add_into(self.held[s][way], self.slots.at[way, s - 2])
            self.copies[s][way].start()

    def finish(self):
        for s in (5, 6):
            for way in range(2):
                self.copies[s][way].wait_recv()
        add_into(self.chunk(self.at, 0), self.slots.at[0, 6], self.slots.at[1, 5])
        add_into(self.chunk(self.at, 1), self.slots.at[0, 5], self.slots.at[1, 6])

    def close(self):
        for pair in self.copies:
            for c in pair:
                c.wait_send()


class Group:
    def __init__(self, where, part, ar, ac, first, sizes, buf, sem):
        (row, col, x, y, zhi, zlo, core), (at_x, at_y, at_z, other) = where
        z = zhi * 4 + zlo
        nx, ny, nz = sizes
        xr, yr, zr = pl.ds(first, nx), pl.ds(first + nx, ny), pl.ds(first + nx + ny, nz)
        self.xy, self.zr, self.all = pl.ds(first, nx + ny), zr, pl.ds(first, nx + ny + nz)
        self.where, self.part, self.ar, self.ac, self.sem, self.buf = where, part, ar, ac, sem, buf
        xp, xm, yp, ym, zp, zm = at_x(x + 1), at_x(x + 3), at_y(y + 1), at_y(y + 3), at_z(z + 1), at_z(z + 7)
        quarter = lambda h: pl.ds(2 * h, 2)
        ring = lambda k, i, plus, minus, chunk: Ring4(i, plus, minus, chunk, buf[2 * k], buf[2 * k + 1], sem[k].at[0], sem[k].at[1])
        near, far = pl.ds(zlo // 2 * 2, 2), pl.ds(2 - zlo // 2 * 2, 2)
        self.x1n = ring(0, x, xp, xm, lambda i, h: part.at[i, :, h, near, xr])
        self.x1f = ring(1, x, xp, xm, lambda i, h: part.at[i, :, h, far, xr])
        self.y1n = ring(2, y, yp, ym, lambda i, h: part.at[:, i, h, near, yr])
        self.y1f = ring(3, y, yp, ym, lambda i, h: part.at[:, i, h, far, yr])
        self.x2n = ring(4, y, yp, ym, lambda i, h: part.at[x, i, h, near, xr])
        self.x2f = ring(5, y, yp, ym, lambda i, h: part.at[x, i, h, far, xr])
        self.y2n = ring(6, x, xp, xm, lambda i, h: part.at[i, y, h, near, yr])
        self.y2f = ring(7, x, xp, xm, lambda i, h: part.at[i, y, h, far, yr])
        self.z2 = ring(8, x, xp, xm, lambda i, h: part.at[i, quarter(h), zhi, zlo, zr])
        self.z1 = Ring8(z, zp, zm, lambda i, h: part.at[quarter(h), :, i // 4, i % 4, zr], buf[18], sem[9].at[0], sem[9].at[1])
        self.last_z = [
            copy_to(at_z(z + k), part.at[x, y, (z + k) % 8 // 4, (z + k) % 4, self.xy], buf[19].at[k - 1], sem[10].at[0, k], sem[10].at[1, k])
            for k in range(1, 8)
        ]
        self.last_y = [
            copy_to(at_y(y + k), part.at[x, (y + k) % 4, zhi, zlo, zr], buf[20].at[k - 1], sem[11].at[0, k], sem[11].at[1, k])
            for k in range(1, 4)
        ]

    def finish_sums(self):
        (row, col, x, y, zhi, zlo, core), _ = self.where
        for rows, copies, slots in ((self.zr, self.last_y, self.buf[20]), (self.xy, self.last_z, self.buf[19])):
            total = self.part[x, y, zhi, zlo, rows]
            for k, c in enumerate(copies):
                c.wait_recv()
                total = total + slots[k]
            self.ar[col, rows] = total

    def near(self, there, device, k):
        view = self.ar.at[there, self.all]
        return copy_to(device, view, view, self.sem[12].at[0, k], self.sem[12].at[1, k])

    def near_send(self, k):
        (row, col, x, y, zhi, zlo, core), _ = self.where
        return self.near(col, (row, y * 4 + (zlo + k) % 4), k)

    def near_recv(self, k):
        (row, col, x, y, zhi, zlo, core), _ = self.where
        there = y * 4 + (zlo + 4 - k) % 4
        return self.near(there, (row, there), k)

    def along_y(self, there, j, k):
        (row, col, x, y, zhi, zlo, core), (at_x, at_y, at_z, other) = self.where
        view = self.ar.at[there, self.all]
        return copy_to(at_y(y + k), view, view, self.sem[13].at[0, j, k], self.sem[13].at[1, j, k])

    def along_y_send(self, j, k):
        (row, col, x, y, zhi, zlo, core), _ = self.where
        return self.along_y(y * 4 + (zlo + 4 - j) % 4, j, k)

    def along_y_recv(self, j, k):
        (row, col, x, y, zhi, zlo, core), _ = self.where
        return self.along_y(((y + 4 - k) % 4) * 4 + (zlo + 4 - j) % 4, j, k)

    def across(self, i):
        (row, col, x, y, zhi, zlo, core), _ = self.where
        device = (((x + i // 2) % 4) * 4 + ((zhi + i % 2) % 2) * 2 + zlo % 2, row)
        return copy_to(device, self.ar.at[col, self.all], self.ac.at[col, self.all], self.sem[14].at[i], self.sem[15].at[col // 2])

    def stay(self):
        (row, col, x, y, zhi, zlo, core), _ = self.where
        return pltpu.make_async_copy(self.ar.at[col, self.all], self.ac.at[col, self.all], self.sem[15].at[col // 2])

    def hand(self, s):
        (row, col, x, y, zhi, zlo, core), (at_x, at_y, at_z, other) = self.where
        view = self.ac.at[s, self.all]
        return copy_to(other, view, view, self.sem[16].at[0, s], self.sem[16].at[1, s])

    def start_gather(self):
        (row, col, x, y, zhi, zlo, core), _ = self.where
        for k in range(1, 4):
            self.near_send(k).start()

        @pl.when(row == col)
        def _():
            self.stay().start()

        @pl.when(row != col)
        def _():
            self.across(0).start()

        for k in range(1, 4):
            self.along_y_send(0, k).start()
        for i in range(1, 8):
            self.across(i).start()

    def middle_gather(self):
        for j in range(1, 4):
            self.near_recv(j).wait_recv()
            for k in range(1, 4):
                self.along_y_send(j, k).start()

    def pass_on(self):
        (row, col, x, y, zhi, zlo, core), (at_x, at_y, at_z, other) = self.where

        def body(j, carry):
            s = 2 * j + core
            view = self.ac.at[s, self.all]
            copy_to(other, view, view, self.sem[14].at[0], self.sem[15].at[j]).wait_recv()
            self.hand(s).start()
            return carry

        lax.fori_loop(0, 8, body, 0)

    def finish_gather(self):
        (row, col, x, y, zhi, zlo, core), _ = self.where
        for j in range(4):
            for k in range(1, 4):
                self.along_y_recv(j, k).wait_recv()

        def body(j, carry):
            self.hand(2 * j + 1 - core).wait_recv()
            return carry

        lax.fori_loop(0, 8, body, 0)

    def close_sums(self):
        for ring in (self.x1n, self.x1f, self.y1n, self.y1f, self.z1, self.x2n, self.x2f, self.y2n, self.y2f, self.z2):
            ring.close()
        for c in self.last_z + self.last_y:
            c.wait_send()

    def close_gather(self):
        (row, col, x, y, zhi, zlo, core), _ = self.where
        for k in range(1, 4):
            self.near_send(k).wait_send()
            for j in range(4):
                self.along_y_send(j, k).wait_send()

        @pl.when(row != col)
        def _():
            self.across(0).wait_send()

        for i in range(1, 8):
            self.across(i).wait_send()

        def body(j, carry):
            self.hand(2 * j + core).wait_send()
            return carry

        lax.fori_loop(0, 8, body, 0)


def group_buffers(sizes):
    nx, ny, nz = sizes
    one = lambda *lead: [(2,) + lead, (2, 2) + lead]
    shapes = one(4, 2, nx) * 2 + one(4, 2, ny) * 2 + one(2, nx) * 2 + one(2, ny) * 2 + one(2, nz)
    shapes += [(2, 7, 2, 4, nz), (7, nx + ny), (3, nz)]
    return [pltpu.VMEM(s + (128,), jnp.float32) for s in shapes]


def group_sems():
    shapes = [(2, 6)] * 9 + [(2, 2, 7), (2, 8), (2, 4), (2, 4), (2, 4, 4), (8,), (8,), (2, 16)]
    return [pltpu.SemaphoreType.DMA(s) for s in shapes]


def kernel(
    surf, eig, levels_in, energies_in, amp_out, r_out, s_raw, s_buf, v_buf, part, ar, ac, pole, levels, energies,
    loc_sem, s_send, s_recv, a_send, a_recv, f_send, f_recv, *rest,
):
    row, col = lax.axis_index("row"), lax.axis_index("col")
    x, zhi, core = row // 4, (row // 2) % 2, row % 2
    y, zlo = col // 4, col % 4
    z = zhi * 4 + zlo
    other = (row + 1 - 2 * core, col)

    def at_x(i):
        return ((i % 4) * 4 + zhi * 2 + core, col)

    def at_y(i):
        return (row, (i % 4) * 4 + zlo)

    def at_z(i):
        i = i % 8
        return (x * 4 + (i // 4) * 2 + core, y * 4 + i % 4)

    def load_s(i):
        return pltpu.make_async_copy(surf.at[:, columns(2 * i + core)], s_raw.at[0, i], loc_sem.at[i])

    def give_s(i):
        return copy_to(other, surf.at[:, columns(2 * i + 1 - core)], s_raw.at[1, i], s_send.at[i], s_recv.at[i])

    def columns(i):
        return pl.ds(pl.multiple_of(128 * i, 128), 128)

    for i in range(8):
        load_s(i).start()
    load_levels = pltpu.make_async_copy(levels_in, levels, loc_sem.at[9])
    load_levels.start()
    load_energies = pltpu.make_async_copy(energies_in, energies, loc_sem.at[10])
    load_energies.start()
    load_v = pltpu.make_async_copy(eig.at[col], v_buf.at[0, 0], loc_sem.at[8])
    load_v.start()

    barrier = pltpu.get_barrier_semaphore()

    def greet(device):
        pl.semaphore_signal(barrier, inc=1, device_id=device, device_id_type=MESH)

    def greet_col(j, carry):
        greet((row, ((y + j // 4) % 4) * 4 + (zlo + j % 4) % 4))
        return carry

    lax.fori_loop(1, 16, greet_col, 0)
    greet(other)
    greet(at_x(x + 1))
    greet(at_x(x + 3))

    def greet_z(j, carry):
        greet((x * 4 + (1 - zhi) * 2 + core, y * 4 + j))
        return carry

    lax.fori_loop(0, 4, greet_z, 0)

    def greet_t2(j, carry):
        source = 2 * j + core

        @pl.when(jnp.logical_or(row != col, source != col))
        def _():
            greet((col, source))

        return carry

    lax.fori_loop(0, 8, greet_t2, 0)
    diagonal = row == col
    pl.semaphore_wait(barrier, jnp.where(diagonal, 29, 30))

    def a2a(j):
        dest = ((y + j % 4) % 4) * 4 + apart(j // 4)
        return copy_to((row, dest), eig.at[dest], v_buf.at[0, j], a_send.at[j], a_recv.at[j])

    def apart(k):
        low, high = (zlo + k) % 2, (zlo // 2 + k // 2) % 2
        return high * 2 + low

    def send_a2a(i, carry):
        a2a((i + 7) % 15 + 1).start()
        return carry

    lax.fori_loop(0, 15, send_a2a, 0)
    for i in range(8):
        give_s(i).start()
    load_levels.wait()
    load_energies.wait()
    for e in range(8):
        pole[e:e + 1] = (1.0 / math.sqrt(2048.0)) / (levels[...] - energies[e])

    def forward(j):
        return copy_to(other, v_buf.at[0, j], v_buf.at[1, j], f_send.at[j], f_recv.at[j])

    load_v.wait()
    forward(0).start()
    for i in range(8):
        load_s(i).wait()
        s_buf[0, 128 * i:128 * i + 128] = s_raw[0, i].T
    for i in range(8):
        give_s(i).wait_recv()
        s_buf[1, 128 * i:128 * i + 128] = s_raw[1, i].T

    def multiply(i):
        zs = apart(i // 2)
        got = None
        for q in range(2):
            two = jnp.concatenate([v_buf[q, 2 * i], v_buf[q, 2 * i + 1]], axis=1)
            one = jnp.dot(s_buf[q], two, preferred_element_type=jnp.float32)
            got = one if got is None else got + one
        for h in range(2):
            ys = (y + 4 - (2 * i + h) % 4) % 4
            for xi in range(4):
                for zh in range(2):
                    at = (xi * 2 + zh) * 128
                    part[xi, ys, zh, zs] = got[at:at + 128, h * 128:h * 128 + 128]

    def take(j):
        a2a(j).wait_recv()
        forward(j).start()

    where = (row, col, x, y, zhi, zlo, core), (at_x, at_y, at_z, other)
    groups, first, per = [], 0, len(rest) // len(GROUPS)
    for g, sizes in enumerate(GROUPS):
        own = rest[g * per:(g + 1) * per]
        groups.append(Group(where, part, ar, ac, first, sizes, own[:21], own[21:]))
        first += sum(sizes)
    def step(i, carry):
        take(2 * i)
        take(2 * i + 1)
        forward(2 * i - 2).wait_recv()
        forward(2 * i - 1).wait_recv()
        multiply(i - 1)
        return carry

    def drain(i):
        forward(2 * i).wait_recv()
        forward(2 * i + 1).wait_recv()
        multiply(i)

    take(1)
    lax.fori_loop(1, 4, step, 0)
    drain(3)
    a, b = groups
    a.x1n.start()
    a.y1n.start()
    a.x1n.middle()
    b.x1n.start()
    a.y1n.middle()
    b.y1n.start()
    a.x1n.finish()
    a.x2n.start()
    take(8)
    take(9)
    lax.fori_loop(5, 7, step, 0)
    b.x1n.middle()
    a.y1n.finish()
    a.y2n.start()
    b.y1n.middle()
    b.x1n.finish()
    a.y2n.middle()
    b.x2n.start()
    a.x2n.middle()
    lax.fori_loop(7, 8, step, 0)
    drain(7)
    a.x1f.start()
    a.y1f.start()
    a.z1.start()
    a.y2n.finish()
    b.y1n.finish()
    b.y2n.start()
    b.x2n.middle()
    a.z1.step(2)
    a.z1.step(3)
    a.x1f.middle()
    b.x1f.start()
    a.x2n.finish()
    a.z1.step(4)
    a.z1.step(5)
    b.z1.start()
    a.y1f.middle()
    b.y2n.middle()
    b.y1f.start()
    a.z1.step(6)
    b.x2n.finish()
    a.x1f.finish()
    a.x2f.start()
    b.z1.step(2)
    a.y1f.finish()
    a.y2f.start()
    b.z1.step(3)
    b.x1f.middle()
    b.y1f.middle()
    a.z1.finish()
    a.z2.start()
    a.x2f.middle()
    b.z1.step(4)
    b.y2n.finish()
    a.y2f.middle()
    b.z1.step(5)
    b.y1f.finish()
    b.y2f.start()
    a.x2f.finish()
    b.z1.step(6)
    b.x1f.finish()
    a.z2.middle()
    b.x2f.start()
    a.y2f.finish()
    for copy in a.last_z:
        copy.start()
    b.y2f.middle()
    a.z2.finish()
    for copy in a.last_y:
        copy.start()
    b.x2f.middle()
    b.y2f.finish()
    b.z1.finish()
    b.z2.start()
    b.x2f.finish()
    b.z2.middle()
    for copy in b.last_z:
        copy.start()
    b.z2.finish()
    for copy in b.last_y:
        copy.start()
    a.finish_sums()
    a.start_gather()
    b.finish_sums()
    b.start_gather()
    a.middle_gather()
    a.pass_on()
    b.middle_gather()
    a.finish_gather()
    b.pass_on()
    b.finish_gather()
    amp_out[...] = ar[col]


    r_out[...] = jnp.zeros_like(r_out)

    def pair(i, carry):
        a = jnp.concatenate([ar[2 * i], ar[2 * i + 1]], axis=1)
        b = jnp.concatenate([ac[2 * i], ac[2 * i + 1]], axis=1)
        b_hi = b.astype(jnp.bfloat16)
        b_lo = (b - b_hi.astype(jnp.float32)).astype(jnp.bfloat16)
        both = jnp.concatenate([b_hi, b_lo], axis=0)
        p = pole[:, pl.ds(pl.multiple_of(256 * i, 256), 256)]
        his, los = [], []
        for e in range(8):
            scaled = a * p[e:e + 1]
            hi = scaled.astype(jnp.bfloat16)
            his.append(hi)
            los.append((scaled - hi.astype(jnp.float32)).astype(jnp.bfloat16))
        hi = jnp.concatenate(his, axis=0)
        lo = jnp.concatenate(los, axis=0)
        contract = (((1,), (1,)), ((), ()))
        one = lax.dot_general(hi, both, contract, preferred_element_type=jnp.float32)
        two = lax.dot_general(lo, b_hi, contract, preferred_element_type=jnp.float32)
        r_out[...] += (one[:, :128] + (one[:, 128:] + two)).reshape(8, 128, 128)
        return carry

    lax.fori_loop(0, 8, pair, 0)

    def close_a2a(j, carry):
        a2a(j).wait_send()
        return carry

    lax.fori_loop(1, 16, close_a2a, 0)

    def close_forward(j, carry):
        forward(j).wait_send()
        return carry

    lax.fori_loop(0, 16, close_forward, 0)
    for i in range(8):
        give_s(i).wait_send()
    for g in groups:
        g.close_sums()
        g.close_gather()


def local(surface, eigvec, eig_energy, energies):
    width = surface.shape[1]
    f32, bf16 = jnp.float32, jnp.bfloat16
    dma = pltpu.SemaphoreType.DMA
    vmem = pl.BlockSpec(memory_space=pltpu.VMEM)
    return pl.pallas_call(
        kernel,
        out_shape=(jax.ShapeDtypeStruct((128, 128), f32), jax.ShapeDtypeStruct((8, 128, 128), f32)),
        in_specs=[pl.BlockSpec(memory_space=pl.ANY)] * 4,
        out_specs=(vmem, vmem),
        scratch_shapes=[
            pltpu.VMEM((2, 8, width, 128), bf16),
            pltpu.VMEM((2, 1024, width), bf16),
            pltpu.VMEM((2, 16, width, 128), bf16),
            pltpu.VMEM((4, 4, 2, 4, 128, 128), f32),
            pltpu.VMEM((16, 128, 128), f32),
            pltpu.VMEM((16, 128, 128), f32),
            pltpu.VMEM((8, 2048), f32),
            pltpu.VMEM((1, 2048), f32),
            pltpu.SMEM((8,), f32),
            dma((11,)), dma((8,)), dma((8,)), dma((16,)), dma((16,)), dma((16,)), dma((16,)),
        ] + [item for sizes in GROUPS for item in group_buffers(sizes) + group_sems()],
        compiler_params=pltpu.CompilerParams(
            collective_id=0, has_side_effects=True, vmem_limit_bytes=60 * 1024 * 1024
        ),
    )(
        surface.T,
        eigvec.reshape(16, width, 128),
        eig_energy.reshape(1, -1),
        energies,
    )


def solution(mesh):
    in_specs = (P(None, ("row", "col")), P("row", "col"), P(), P())
    out_specs = (P("row", "col"), P(None, "row", "col"))
    return jax.shard_map(local, mesh=mesh, in_specs=in_specs, out_specs=out_specs, check_vma=False)
```

```python
import functools
import math

import jax
import jax.numpy as jnp
from jax import lax
from jax.experimental import pallas as pl
from jax.experimental.pallas import tpu as pltpu
from jax.sharding import PartitionSpec as P

MESH = pl.DeviceIdType.MESH
GROUPS = ((56, 48, 24),)


def copy_to(device, src, dst, send, recv):
    return pltpu.make_async_remote_copy(
        src_ref=src, dst_ref=dst, send_sem=send, recv_sem=recv, device_id=device, device_id_type=MESH
    )


def add_into(dst, *srcs):
    shape = dst.shape
    if len(shape) == 2:
        total = dst[...]
        for s in srcs:
            total = total + s[...]
        dst[...] = total
        return
    lead = shape[:-2]
    count = math.prod(lead)

    def body(i, carry):
        at = (i,) if len(lead) == 1 else (i // lead[1], i % lead[1])
        total = dst[at]
        for s in srcs:
            total = total + s[at]
        dst[at] = total
        return carry

    lax.fori_loop(0, count, body, 0)


class Ring4:
    def __init__(self, at, plus, minus, chunk, far, near, send, recv):
        self.at, self.chunk, self.near = at, chunk, near
        up, down, across = (at + 1) % 4, (at + 3) % 4, (at + 2) % 4
        self.up, self.down, self.far = up, down, far
        c = functools.partial
        self.p1 = copy_to(plus, chunk(across, 0), far.at[0], send.at[0], recv.at[0])
        self.m1 = copy_to(minus, chunk(across, 1), far.at[1], send.at[1], recv.at[1])
        self.p2 = copy_to(plus, chunk(up, 1), near.at[0, 1], send.at[2], recv.at[2])
        self.m2 = copy_to(minus, chunk(down, 0), near.at[1, 0], send.at[3], recv.at[3])
        self.p3 = copy_to(plus, chunk(up, 0), near.at[0, 0], send.at[4], recv.at[4])
        self.m3 = copy_to(minus, chunk(down, 1), near.at[1, 1], send.at[5], recv.at[5])

    def start(self):
        for c in (self.p1, self.m1, self.p2, self.m2):
            c.start()

    def middle(self):
        self.p1.wait_recv()
        add_into(self.chunk(self.up, 0), self.far.at[0])
        self.p3.start()
        self.m1.wait_recv()
        add_into(self.chunk(self.down, 1), self.far.at[1])
        self.m3.start()

    def finish(self):
        for c in (self.p2, self.m2, self.p3, self.m3):
            c.wait_recv()
        for h in range(2):
            add_into(self.chunk(self.at, h), self.near.at[0, h], self.near.at[1, h])

    def close(self):
        for c in (self.p1, self.m1, self.p2, self.m2, self.p3, self.m3):
            c.wait_send()


class Ring8:
    def __init__(self, at, plus, minus, chunk, slots, send, recv):
        self.at, self.chunk, self.slots = at, chunk, slots
        self.copies, self.held = [], []
        for s in range(7):
            k = 4 - (s + 1) // 2
            h = 0 if s % 2 == 0 else 1
            pair, held = [], []
            for way, device in ((0, plus), (1, minus)):
                i = (at + k) % 8 if way == 0 else (at + 8 - k) % 8
                half = h if way == 0 else 1 - h
                view = chunk(i, half)
                held.append(view)
                pair.append(copy_to(device, view, slots.at[way, s], send.at[way, s], recv.at[way, s]))
            self.copies.append(pair)
            self.held.append(held)

    def start(self):
        for s in range(2):
            for c in self.copies[s]:
                c.start()

    def step(self, s):
        for way in range(2):
            self.copies[s - 2][way].wait_recv()
            add_into(self.held[s][way], self.slots.at[way, s - 2])
            self.copies[s][way].start()

    def finish(self):
        for s in (5, 6):
            for way in range(2):
                self.copies[s][way].wait_recv()
        add_into(self.chunk(self.at, 0), self.slots.at[0, 6], self.slots.at[1, 5])
        add_into(self.chunk(self.at, 1), self.slots.at[0, 5], self.slots.at[1, 6])

    def close(self):
        for pair in self.copies:
            for c in pair:
                c.wait_send()


class Group:
    def __init__(self, where, part, ar, ac, first, sizes, buf, sem):
        (row, col, x, y, zhi, zlo, core), (at_x, at_y, at_z, other) = where
        z = zhi * 4 + zlo
        nx, ny, nz = sizes
        xr, yr, zr = pl.ds(first, nx), pl.ds(first + nx, ny), pl.ds(first + nx + ny, nz)
        self.xy, self.zr, self.all = pl.ds(first, nx + ny), zr, pl.ds(first, nx + ny + nz)
        self.where, self.part, self.ar, self.ac, self.sem, self.buf = where, part, ar, ac, sem, buf
        xp, xm, yp, ym, zp, zm = at_x(x + 1), at_x(x + 3), at_y(y + 1), at_y(y + 3), at_z(z + 1), at_z(z + 7)
        quarter = lambda h: pl.ds(2 * h, 2)
        ring = lambda k, i, plus, minus, chunk: Ring4(i, plus, minus, chunk, buf[2 * k], buf[2 * k + 1], sem[k].at[0], sem[k].at[1])
        near, far = pl.ds(zlo // 2 * 2, 2), pl.ds(2 - zlo // 2 * 2, 2)
        self.x1n = ring(0, x, xp, xm, lambda i, h: part.at[i, :, h, near, xr])
        self.x1f = ring(1, x, xp, xm, lambda i, h: part.at[i, :, h, far, xr])
        self.y1n = ring(2, y, yp, ym, lambda i, h: part.at[:, i, h, near, yr])
        self.y1f = ring(3, y, yp, ym, lambda i, h: part.at[:, i, h, far, yr])
        self.x2n = ring(4, y, yp, ym, lambda i, h: part.at[x, i, h, near, xr])
        self.x2f = ring(5, y, yp, ym, lambda i, h: part.at[x, i, h, far, xr])
        self.y2n = ring(6, x, xp, xm, lambda i, h: part.at[i, y, h, near, yr])
        self.y2f = ring(7, x, xp, xm, lambda i, h: part.at[i, y, h, far, yr])
        self.z2 = ring(8, x, xp, xm, lambda i, h: part.at[i, quarter(h), zhi, zlo, zr])
        self.z1 = Ring8(z, zp, zm, lambda i, h: part.at[quarter(h), :, i // 4, i % 4, zr], buf[18], sem[9].at[0], sem[9].at[1])
        self.last_z = []
        for k in range(1, 8):
            high, low = (zhi + k // 4) % 2, ((zlo // 2 + k // 2) % 2) * 2 + (zlo + k) % 2
            self.last_z.append(copy_to(
                (x * 4 + high * 2 + core, y * 4 + low), part.at[x, y, high, low, self.xy], buf[19].at[k - 1],
                sem[10].at[0, k], sem[10].at[1, k],
            ))
        self.last_y = [
            copy_to(at_y(y + k), part.at[x, (y + k) % 4, zhi, zlo, zr], buf[20].at[k - 1], sem[11].at[0, k], sem[11].at[1, k])
            for k in range(1, 4)
        ]

    def start_last_z(self, near):
        for k in range(1, 8):
            if (k in (1, 4, 5)) == near:
                self.last_z[k - 1].start()

    def start_last_y(self):
        for c in self.last_y:
            c.start()

    def finish_sums(self):
        (row, col, x, y, zhi, zlo, core), _ = self.where
        for rows, copies, slots in ((self.zr, self.last_y, self.buf[20]), (self.xy, self.last_z, self.buf[19])):
            total = self.part[x, y, zhi, zlo, rows]
            for k, c in enumerate(copies):
                c.wait_recv()
                total = total + slots[k]
            self.ar[col, rows] = total

    def near(self, there, device, k):
        view = self.ar.at[there, self.all]
        return copy_to(device, view, view, self.sem[12].at[0, k], self.sem[12].at[1, k])

    def near_send(self, k):
        (row, col, x, y, zhi, zlo, core), _ = self.where
        return self.near(col, (row, y * 4 + (zlo + k) % 4), k)

    def near_recv(self, k):
        (row, col, x, y, zhi, zlo, core), _ = self.where
        there = y * 4 + (zlo + 4 - k) % 4
        return self.near(there, (row, there), k)

    def along_y(self, there, j, k):
        (row, col, x, y, zhi, zlo, core), (at_x, at_y, at_z, other) = self.where
        view = self.ar.at[there, self.all]
        return copy_to(at_y(y + k), view, view, self.sem[13].at[0, j, k], self.sem[13].at[1, j, k])

    def along_y_send(self, j, k):
        (row, col, x, y, zhi, zlo, core), _ = self.where
        return self.along_y(y * 4 + (zlo + 4 - j) % 4, j, k)

    def along_y_recv(self, j, k):
        (row, col, x, y, zhi, zlo, core), _ = self.where
        return self.along_y(((y + 4 - k) % 4) * 4 + (zlo + 4 - j) % 4, j, k)

    def across(self, i):
        (row, col, x, y, zhi, zlo, core), _ = self.where
        device = (((x + i // 2) % 4) * 4 + ((zhi + i % 2) % 2) * 2 + zlo % 2, row)
        return copy_to(device, self.ar.at[col, self.all], self.ac.at[col, self.all], self.sem[14].at[i], self.sem[15].at[col // 2])

    def stay(self):
        (row, col, x, y, zhi, zlo, core), _ = self.where
        return pltpu.make_async_copy(self.ar.at[col, self.all], self.ac.at[col, self.all], self.sem[15].at[col // 2])

    def hand(self, s):
        (row, col, x, y, zhi, zlo, core), (at_x, at_y, at_z, other) = self.where
        view = self.ac.at[s, self.all]
        return copy_to(other, view, view, self.sem[16].at[0, s], self.sem[16].at[1, s])

    def start_gather(self):
        (row, col, x, y, zhi, zlo, core), _ = self.where
        for k in range(1, 4):
            self.near_send(k).start()

        @pl.when(row == col)
        def _():
            self.stay().start()

        @pl.when(row != col)
        def _():
            self.across(0).start()

        for k in range(1, 4):
            self.along_y_send(0, k).start()
        for i in range(1, 8):
            self.across(i).start()

    def middle_gather(self):
        for j in range(1, 4):
            self.near_recv(j).wait_recv()
            for k in range(1, 4):
                self.along_y_send(j, k).start()

    def pass_on(self):
        (row, col, x, y, zhi, zlo, core), (at_x, at_y, at_z, other) = self.where

        def body(j, carry):
            s = 2 * j + core
            view = self.ac.at[s, self.all]
            copy_to(other, view, view, self.sem[14].at[0], self.sem[15].at[j]).wait_recv()
            self.hand(s).start()
            return carry

        lax.fori_loop(0, 8, body, 0)

    def finish_gather(self):
        (row, col, x, y, zhi, zlo, core), _ = self.where
        for j in range(4):
            for k in range(1, 4):
                self.along_y_recv(j, k).wait_recv()

        def body(j, carry):
            self.hand(2 * j + 1 - core).wait_recv()
            return carry

        lax.fori_loop(0, 8, body, 0)

    def close_sums(self):
        for ring in (self.x1n, self.x1f, self.y1n, self.y1f, self.z1, self.x2n, self.x2f, self.y2n, self.y2f, self.z2):
            ring.close()
        for c in self.last_z + self.last_y:
            c.wait_send()

    def close_gather(self):
        (row, col, x, y, zhi, zlo, core), _ = self.where
        for k in range(1, 4):
            self.near_send(k).wait_send()
            for j in range(4):
                self.along_y_send(j, k).wait_send()

        @pl.when(row != col)
        def _():
            self.across(0).wait_send()

        for i in range(1, 8):
            self.across(i).wait_send()

        def body(j, carry):
            self.hand(2 * j + core).wait_send()
            return carry

        lax.fori_loop(0, 8, body, 0)


def group_buffers(sizes):
    nx, ny, nz = sizes
    one = lambda *lead: [(2,) + lead, (2, 2) + lead]
    shapes = one(4, 2, nx) * 2 + one(4, 2, ny) * 2 + one(2, nx) * 2 + one(2, ny) * 2 + one(2, nz)
    shapes += [(2, 7, 2, 4, nz), (7, nx + ny), (3, nz)]
    return [pltpu.VMEM(s + (128,), jnp.float32) for s in shapes]


def group_sems():
    shapes = [(2, 6)] * 9 + [(2, 2, 7), (2, 8), (2, 4), (2, 4), (2, 4, 4), (8,), (8,), (2, 16)]
    return [pltpu.SemaphoreType.DMA(s) for s in shapes]


def kernel(
    surf, eig, poles, amp_out, r_out, s_raw, s_buf, v_buf, part, ar, ac,
    loc_sem, s_send, s_recv, a_send, a_recv, f_send, f_recv, *rest,
):
    row, col = lax.axis_index("row"), lax.axis_index("col")
    x, zhi, core = row // 4, (row // 2) % 2, row % 2
    y, zlo = col // 4, col % 4
    z = zhi * 4 + zlo
    other = (row + 1 - 2 * core, col)

    def at_x(i):
        return ((i % 4) * 4 + zhi * 2 + core, col)

    def at_y(i):
        return (row, (i % 4) * 4 + zlo)

    def at_z(i):
        i = i % 8
        return (x * 4 + (i // 4) * 2 + core, y * 4 + i % 4)

    def load_s(i):
        return pltpu.make_async_copy(surf.at[:, columns(2 * i + core)], s_raw.at[0, i], loc_sem.at[i])

    def give_s(i):
        return copy_to(other, surf.at[:, columns(2 * i + 1 - core)], s_raw.at[1, i], s_send.at[i], s_recv.at[i])

    def columns(i):
        return pl.ds(pl.multiple_of(128 * i, 128), 128)

    for i in range(8):
        load_s(i).start()
    load_v = pltpu.make_async_copy(eig.at[col], v_buf.at[0, 0], loc_sem.at[8])
    load_v.start()

    barrier = pltpu.get_barrier_semaphore()

    def greet(device):
        pl.semaphore_signal(barrier, inc=1, device_id=device, device_id_type=MESH)

    def greet_col(j, carry):
        greet((row, ((y + j // 4) % 4) * 4 + (zlo + j % 4) % 4))
        return carry

    lax.fori_loop(1, 16, greet_col, 0)
    greet(other)
    greet(at_x(x + 1))
    greet(at_x(x + 3))

    greet(at_z(z + 1))
    greet(at_z(z + 7))
    pl.semaphore_wait(barrier, 20)

    def a2a(j):
        dest = ((y + j % 4) % 4) * 4 + apart(j // 4)
        return copy_to((row, dest), eig.at[dest], v_buf.at[0, j], a_send.at[j], a_recv.at[j])

    def apart(k):
        low, high = (zlo + k) % 2, (zlo // 2 + k // 2) % 2
        return high * 2 + low

    def send_a2a(i, carry):
        a2a(i + 1).start()
        return carry

    lax.fori_loop(0, 15, send_a2a, 0)
    for i in range(8):
        give_s(i).start()
    def forward(j):
        return copy_to(other, v_buf.at[0, j], v_buf.at[1, j], f_send.at[j], f_recv.at[j])

    load_v.wait()
    forward(0).start()
    for i in range(8):
        load_s(i).wait()
        s_buf[0, 128 * i:128 * i + 128] = s_raw[0, i].T
    for i in range(8):
        give_s(i).wait_recv()
        s_buf[1, 128 * i:128 * i + 128] = s_raw[1, i].T

    def multiply(i):
        zs = apart(i // 2)
        got = None
        for q in range(2):
            two = jnp.concatenate([v_buf[q, 2 * i], v_buf[q, 2 * i + 1]], axis=1)
            one = jnp.dot(s_buf[q], two, preferred_element_type=jnp.float32)
            got = one if got is None else got + one
        for h in range(2):
            ys = (y + 4 - (2 * i + h) % 4) % 4
            for xi in range(4):
                for zh in range(2):
                    at = (xi * 2 + zh) * 128
                    part[xi, ys, zh, zs] = got[at:at + 128, h * 128:h * 128 + 128]

    def take(j):
        a2a(j).wait_recv()
        forward(j).start()

    where = (row, col, x, y, zhi, zlo, core), (at_x, at_y, at_z, other)
    groups, first, per = [], 0, len(rest) // len(GROUPS)
    for g, sizes in enumerate(GROUPS):
        own = rest[g * per:(g + 1) * per]
        groups.append(Group(where, part, ar, ac, first, sizes, own[:21], own[21:]))
        first += sum(sizes)
    def step(i, carry):
        take(2 * i)
        take(2 * i + 1)
        forward(2 * i - 2).wait_recv()
        forward(2 * i - 1).wait_recv()
        multiply(i - 1)
        return carry

    def drain(i):
        forward(2 * i).wait_recv()
        forward(2 * i + 1).wait_recv()
        multiply(i)

    take(1)
    lax.fori_loop(1, 4, step, 0)
    drain(3)
    a, = groups
    a.x1n.start()
    a.y1n.start()
    a.x1n.middle()
    a.y1n.middle()
    take(8)
    take(9)
    lax.fori_loop(5, 7, step, 0)
    a.x1n.finish()
    a.x2n.start()
    lax.fori_loop(7, 8, step, 0)
    drain(7)
    a.x1f.start()
    a.y1f.start()
    a.z1.start()
    a.y1n.finish()
    a.y2n.start()
    a.z1.step(2)
    a.x2n.middle()
    a.z1.step(3)
    a.x1f.middle()
    a.z1.step(4)
    a.z1.step(5)
    a.y1f.middle()
    a.y2n.middle()
    a.z1.step(6)
    a.x2n.finish()
    a.x1f.finish()
    a.z1.finish()
    a.y2n.finish()
    a.x2f.start()
    a.z2.start()
    a.start_last_z(True)
    a.y1f.finish()
    a.y2f.start()
    a.z2.middle()
    a.x2f.middle()
    a.y2f.middle()
    a.z2.finish()
    a.x2f.finish()
    a.start_last_y()
    a.y2f.finish()
    a.start_last_z(False)
    a.finish_sums()
    a.start_gather()
    a.middle_gather()
    a.pass_on()
    a.finish_gather()
    amp_out[...] = ar[col]


    r_out[...] = jnp.zeros_like(r_out)

    def pair(i, carry):
        a = jnp.concatenate([ar[2 * i], ar[2 * i + 1]], axis=1)
        b = jnp.concatenate([ac[2 * i], ac[2 * i + 1]], axis=1)
        b_hi = b.astype(jnp.bfloat16)
        b_lo = (b - b_hi.astype(jnp.float32)).astype(jnp.bfloat16)
        both = jnp.concatenate([b_hi, b_lo], axis=0)
        p = poles[:, pl.ds(pl.multiple_of(256 * i, 256), 256)]
        his, los = [], []
        for e in range(8):
            scaled = a * p[e:e + 1]
            hi = scaled.astype(jnp.bfloat16)
            his.append(hi)
            los.append((scaled - hi.astype(jnp.float32)).astype(jnp.bfloat16))
        hi = jnp.concatenate(his, axis=0)
        lo = jnp.concatenate(los, axis=0)
        contract = (((1,), (1,)), ((), ()))
        one = lax.dot_general(hi, both, contract, preferred_element_type=jnp.float32)
        two = lax.dot_general(lo, b_hi, contract, preferred_element_type=jnp.float32)
        r_out[...] += (one[:, :128] + (one[:, 128:] + two)).reshape(8, 128, 128)
        return carry

    lax.fori_loop(0, 8, pair, 0)

    def close_a2a(j, carry):
        a2a(j).wait_send()
        return carry

    lax.fori_loop(1, 16, close_a2a, 0)

    def close_forward(j, carry):
        forward(j).wait_send()
        return carry

    lax.fori_loop(0, 16, close_forward, 0)
    for i in range(8):
        give_s(i).wait_send()
    for g in groups:
        g.close_sums()
        g.close_gather()


def local(surface, eigvec, eig_energy, energies):
    width = surface.shape[1]
    f32, bf16 = jnp.float32, jnp.bfloat16
    dma = pltpu.SemaphoreType.DMA
    vmem = pl.BlockSpec(memory_space=pltpu.VMEM)
    return pl.pallas_call(
        kernel,
        out_shape=(jax.ShapeDtypeStruct((128, 128), f32), jax.ShapeDtypeStruct((8, 128, 128), f32)),
        in_specs=[pl.BlockSpec(memory_space=pl.ANY)] * 2 + [vmem],
        out_specs=(vmem, vmem),
        scratch_shapes=[
            pltpu.VMEM((2, 8, width, 128), bf16),
            pltpu.VMEM((2, 1024, width), bf16),
            pltpu.VMEM((2, 16, width, 128), bf16),
            pltpu.VMEM((4, 4, 2, 4, 128, 128), f32),
            pltpu.VMEM((16, 128, 128), f32),
            pltpu.VMEM((16, 128, 128), f32),
            dma((9,)), dma((8,)), dma((8,)), dma((16,)), dma((16,)), dma((16,)), dma((16,)),
        ] + [item for sizes in GROUPS for item in group_buffers(sizes) + group_sems()],
        compiler_params=pltpu.CompilerParams(
            collective_id=0, has_side_effects=True, vmem_limit_bytes=52 * 1024 * 1024
        ),
    )(
        surface.T,
        eigvec.reshape(16, width, 128),
        (1.0 / math.sqrt(2048.0)) / (eig_energy[None, :] - energies[:, None]),
    )


def solution(mesh):
    in_specs = (P(None, ("row", "col")), P("row", "col"), P(), P())
    out_specs = (P("row", "col"), P(None, "row", "col"))
    return jax.shard_map(local, mesh=mesh, in_specs=in_specs, out_specs=out_specs, check_vma=False)
```

```python
import functools
import math

import jax
import jax.numpy as jnp
from jax import lax
from jax.experimental import pallas as pl
from jax.experimental.pallas import tpu as pltpu
from jax.sharding import PartitionSpec as P

MESH = pl.DeviceIdType.MESH
GROUPS = ((56, 48, 24),)


def copy_to(device, src, dst, send, recv):
    return pltpu.make_async_remote_copy(
        src_ref=src, dst_ref=dst, send_sem=send, recv_sem=recv, device_id=device, device_id_type=MESH
    )


def add_into(dst, *srcs):
    shape = dst.shape
    if len(shape) == 2:
        total = dst[...]
        for s in srcs:
            total = total + s[...]
        dst[...] = total
        return
    lead = shape[:-2]
    count = math.prod(lead)

    def body(i, carry):
        at = (i,) if len(lead) == 1 else (i // lead[1], i % lead[1])
        total = dst[at]
        for s in srcs:
            total = total + s[at]
        dst[at] = total
        return carry

    lax.fori_loop(0, count, body, 0)


class Ring4:
    def __init__(self, at, plus, minus, chunk, far, near, send, recv):
        self.at, self.chunk, self.near = at, chunk, near
        up, down, across = (at + 1) % 4, (at + 3) % 4, (at + 2) % 4
        self.up, self.down, self.far = up, down, far
        c = functools.partial
        self.p1 = copy_to(plus, chunk(across, 0), far.at[0], send.at[0], recv.at[0])
        self.m1 = copy_to(minus, chunk(across, 1), far.at[1], send.at[1], recv.at[1])
        self.p2 = copy_to(plus, chunk(up, 1), near.at[0, 1], send.at[2], recv.at[2])
        self.m2 = copy_to(minus, chunk(down, 0), near.at[1, 0], send.at[3], recv.at[3])
        self.p3 = copy_to(plus, chunk(up, 0), near.at[0, 0], send.at[4], recv.at[4])
        self.m3 = copy_to(minus, chunk(down, 1), near.at[1, 1], send.at[5], recv.at[5])

    def start(self):
        for c in (self.p1, self.m1, self.p2, self.m2):
            c.start()

    def middle(self):
        self.p1.wait_recv()
        add_into(self.chunk(self.up, 0), self.far.at[0])
        self.p3.start()
        self.m1.wait_recv()
        add_into(self.chunk(self.down, 1), self.far.at[1])
        self.m3.start()

    def finish(self):
        for c in (self.p2, self.m2, self.p3, self.m3):
            c.wait_recv()
        for h in range(2):
            add_into(self.chunk(self.at, h), self.near.at[0, h], self.near.at[1, h])

    def close(self):
        for c in (self.p1, self.m1, self.p2, self.m2, self.p3, self.m3):
            c.wait_send()


class Ring8:
    def __init__(self, at, plus, minus, chunk, slots, send, recv):
        self.at, self.chunk, self.slots = at, chunk, slots
        self.copies, self.held = [], []
        for s in range(7):
            k = 4 - (s + 1) // 2
            h = 0 if s % 2 == 0 else 1
            pair, held = [], []
            for way, device in ((0, plus), (1, minus)):
                i = (at + k) % 8 if way == 0 else (at + 8 - k) % 8
                half = h if way == 0 else 1 - h
                view = chunk(i, half)
                held.append(view)
                pair.append(copy_to(device, view, slots.at[way, s], send.at[way, s], recv.at[way, s]))
            self.copies.append(pair)
            self.held.append(held)

    def start(self):
        for s in range(2):
            for c in self.copies[s]:
                c.start()

    def step(self, s):
        for way in range(2):
            self.copies[s - 2][way].wait_recv()
            add_into(self.held[s][way], self.slots.at[way, s - 2])
            self.copies[s][way].start()

    def finish(self):
        for s in (5, 6):
            for way in range(2):
                self.copies[s][way].wait_recv()
        add_into(self.chunk(self.at, 0), self.slots.at[0, 6], self.slots.at[1, 5])
        add_into(self.chunk(self.at, 1), self.slots.at[0, 5], self.slots.at[1, 6])

    def close(self):
        for pair in self.copies:
            for c in pair:
                c.wait_send()


class Group:
    def __init__(self, where, part, ar, ac, first, sizes, buf, sem):
        (row, col, x, y, zhi, zlo, core), (at_x, at_y, at_z, other) = where
        z = zhi * 4 + zlo
        nx, ny, nz = sizes
        xr, yr, zr = pl.ds(first, nx), pl.ds(first + nx, ny), pl.ds(first + nx + ny, nz)
        self.xy, self.zr, self.all = pl.ds(first, nx + ny), zr, pl.ds(first, nx + ny + nz)
        self.where, self.part, self.ar, self.ac, self.sem, self.buf = where, part, ar, ac, sem, buf
        xp, xm, yp, ym, zp, zm = at_x(x + 1), at_x(x + 3), at_y(y + 1), at_y(y + 3), at_z(z + 1), at_z(z + 7)
        quarter = lambda h: pl.ds(2 * h, 2)
        ring = lambda k, i, plus, minus, chunk: Ring4(i, plus, minus, chunk, buf[2 * k], buf[2 * k + 1], sem[k].at[0], sem[k].at[1])
        near = pl.ds(zlo // 2 * 2, 2)
        mid, far = (zlo + 2) % 4, (zlo // 2 + 1) % 2 * 2 + (zlo + 1) % 2
        self.x1n = ring(0, x, xp, xm, lambda i, h: part.at[i, :, h, near, xr])
        self.x1m = ring(1, x, xp, xm, lambda i, h: part.at[i, :, h, mid, xr])
        self.x1f = ring(2, x, xp, xm, lambda i, h: part.at[i, :, h, far, xr])
        self.y1n = ring(3, y, yp, ym, lambda i, h: part.at[:, i, h, near, yr])
        self.y1m = ring(4, y, yp, ym, lambda i, h: part.at[:, i, h, mid, yr])
        self.y1f = ring(5, y, yp, ym, lambda i, h: part.at[:, i, h, far, yr])
        self.x2n = ring(6, y, yp, ym, lambda i, h: part.at[x, i, h, near, xr])
        self.x2m = ring(7, y, yp, ym, lambda i, h: part.at[x, i, h, mid, xr])
        self.x2f = ring(8, y, yp, ym, lambda i, h: part.at[x, i, h, far, xr])
        self.y2n = ring(9, x, xp, xm, lambda i, h: part.at[i, y, h, near, yr])
        self.y2m = ring(10, x, xp, xm, lambda i, h: part.at[i, y, h, mid, yr])
        self.y2f = ring(11, x, xp, xm, lambda i, h: part.at[i, y, h, far, yr])
        self.z2 = ring(12, x, xp, xm, lambda i, h: part.at[i, quarter(h), zhi, zlo, zr])
        self.rings = (
            self.x1n, self.x1m, self.x1f, self.y1n, self.y1m, self.y1f,
            self.x2n, self.x2m, self.x2f, self.y2n, self.y2m, self.y2f, self.z2,
        )
        self.z1 = Ring8(z, zp, zm, lambda i, h: part.at[quarter(h), :, i // 4, i % 4, zr], buf[26], sem[13].at[0], sem[13].at[1])
        self.last_z = []
        for k in range(1, 8):
            high, low = (zhi + k // 4) % 2, ((zlo // 2 + k // 2) % 2) * 2 + (zlo + k) % 2
            self.last_z.append(copy_to(
                (x * 4 + high * 2 + core, y * 4 + low), part.at[x, y, high, low, self.xy], buf[27].at[k - 1],
                sem[14].at[0, k], sem[14].at[1, k],
            ))
        self.last_y = [
            copy_to(at_y(y + k), part.at[x, (y + k) % 4, zhi, zlo, zr], buf[28].at[k - 1], sem[15].at[0, k], sem[15].at[1, k])
            for k in range(1, 4)
        ]

    def start_last_z(self, *ks):
        for k in ks:
            self.last_z[k - 1].start()

    def start_last_y(self):
        for c in self.last_y:
            c.start()

    def finish_sums(self):
        (row, col, x, y, zhi, zlo, core), _ = self.where
        for rows, copies, slots in ((self.zr, self.last_y, self.buf[28]), (self.xy, self.last_z, self.buf[27])):
            total = self.part[x, y, zhi, zlo, rows]
            for k, c in enumerate(copies):
                c.wait_recv()
                total = total + slots[k]
            self.ar[col, rows] = total

    def near(self, there, device, k):
        view = self.ar.at[there, self.all]
        return copy_to(device, view, view, self.sem[16].at[0, k], self.sem[16].at[1, k])

    def near_send(self, k):
        (row, col, x, y, zhi, zlo, core), _ = self.where
        return self.near(col, (row, y * 4 + (zlo + k) % 4), k)

    def near_recv(self, k):
        (row, col, x, y, zhi, zlo, core), _ = self.where
        there = y * 4 + (zlo + 4 - k) % 4
        return self.near(there, (row, there), k)

    def along_y(self, there, j, k):
        (row, col, x, y, zhi, zlo, core), (at_x, at_y, at_z, other) = self.where
        view = self.ar.at[there, self.all]
        return copy_to(at_y(y + k), view, view, self.sem[17].at[0, j, k], self.sem[17].at[1, j, k])

    def along_y_send(self, j, k):
        (row, col, x, y, zhi, zlo, core), _ = self.where
        return self.along_y(y * 4 + (zlo + 4 - j) % 4, j, k)

    def along_y_recv(self, j, k):
        (row, col, x, y, zhi, zlo, core), _ = self.where
        return self.along_y(((y + 4 - k) % 4) * 4 + (zlo + 4 - j) % 4, j, k)

    def across(self, i):
        (row, col, x, y, zhi, zlo, core), _ = self.where
        device = (((x + i // 2) % 4) * 4 + ((zhi + i % 2) % 2) * 2 + zlo % 2, row)
        return copy_to(device, self.ar.at[col, self.all], self.ac.at[col, self.all], self.sem[18].at[i], self.sem[19].at[col // 2])

    def stay(self):
        (row, col, x, y, zhi, zlo, core), _ = self.where
        return pltpu.make_async_copy(self.ar.at[col, self.all], self.ac.at[col, self.all], self.sem[19].at[col // 2])

    def hand(self, s):
        (row, col, x, y, zhi, zlo, core), (at_x, at_y, at_z, other) = self.where
        view = self.ac.at[s, self.all]
        return copy_to(other, view, view, self.sem[20].at[0, s], self.sem[20].at[1, s])

    def start_gather(self):
        (row, col, x, y, zhi, zlo, core), _ = self.where
        for k in range(1, 4):
            self.near_send(k).start()

        @pl.when(row == col)
        def _():
            self.stay().start()

        @pl.when(row != col)
        def _():
            self.across(0).start()

        for k in range(1, 4):
            self.along_y_send(0, k).start()
        for i in range(1, 8):
            self.across(i).start()

    def middle_gather(self):
        for j in range(1, 4):
            self.near_recv(j).wait_recv()
            for k in range(1, 4):
                self.along_y_send(j, k).start()

    def pass_on(self, k):
        (row, col, x, y, zhi, zlo, core), (at_x, at_y, at_z, other) = self.where
        for q in range(2):
            s = (y + 4 - k) % 4 * 4 + 2 * q + core
            view = self.ac.at[s, self.all]
            copy_to(other, view, view, self.sem[18].at[0], self.sem[19].at[s // 2]).wait_recv()
            self.hand(s).start()

    def arrive(self, k):
        (row, col, x, y, zhi, zlo, core), _ = self.where
        for j in range(4):
            if k > 0:
                self.along_y_recv(j, k).wait_recv()
        for q in range(2):
            self.hand((y + 4 - k) % 4 * 4 + 2 * q + 1 - core).wait_recv()

    def close_sums(self):
        for ring in self.rings + (self.z1,):
            ring.close()
        for c in self.last_z + self.last_y:
            c.wait_send()

    def close_gather(self):
        (row, col, x, y, zhi, zlo, core), _ = self.where
        for k in range(1, 4):
            self.near_send(k).wait_send()
            for j in range(4):
                self.along_y_send(j, k).wait_send()

        @pl.when(row != col)
        def _():
            self.across(0).wait_send()

        for i in range(1, 8):
            self.across(i).wait_send()

        def body(j, carry):
            self.hand(2 * j + core).wait_send()
            return carry

        lax.fori_loop(0, 8, body, 0)


def group_buffers(sizes):
    nx, ny, nz = sizes
    one = lambda *lead: [(2,) + lead, (2, 2) + lead]
    shapes = one(4, 2, nx) + one(4, nx) * 2 + one(4, 2, ny) + one(4, ny) * 2
    shapes += one(2, nx) + one(nx) * 2 + one(2, ny) + one(ny) * 2 + one(2, nz)
    shapes += [(2, 7, 2, 4, nz), (7, nx + ny), (3, nz)]
    return [pltpu.VMEM(s + (128,), jnp.float32) for s in shapes]


def group_sems():
    shapes = [(2, 6)] * 13 + [(2, 2, 7), (2, 8), (2, 4), (2, 4), (2, 4, 4), (8,), (8,), (2, 16)]
    return [pltpu.SemaphoreType.DMA(s) for s in shapes]


def kernel(
    surf, eig, poles, amp_out, r_out, s_raw, s_buf, v_buf, part, ar, ac,
    loc_sem, s_send, s_recv, a_send, a_recv, f_send, f_recv, *rest,
):
    row, col = lax.axis_index("row"), lax.axis_index("col")
    x, zhi, core = row // 4, (row // 2) % 2, row % 2
    y, zlo = col // 4, col % 4
    z = zhi * 4 + zlo
    other = (row + 1 - 2 * core, col)

    def at_x(i):
        return ((i % 4) * 4 + zhi * 2 + core, col)

    def at_y(i):
        return (row, (i % 4) * 4 + zlo)

    def at_z(i):
        i = i % 8
        return (x * 4 + (i // 4) * 2 + core, y * 4 + i % 4)

    def load_s(i):
        return pltpu.make_async_copy(surf.at[:, columns(2 * i + core)], s_raw.at[0, i], loc_sem.at[i])

    def give_s(i):
        return copy_to(other, surf.at[:, columns(2 * i + 1 - core)], s_raw.at[1, i], s_send.at[i], s_recv.at[i])

    def columns(i):
        return pl.ds(pl.multiple_of(128 * i, 128), 128)

    for i in range(8):
        load_s(i).start()
    load_v = pltpu.make_async_copy(eig.at[col], v_buf.at[0, 0], loc_sem.at[8])
    load_v.start()

    barrier = pltpu.get_barrier_semaphore()

    def greet(device):
        pl.semaphore_signal(barrier, inc=1, device_id=device, device_id_type=MESH)

    def greet_col(j, carry):
        greet((row, ((y + j // 4) % 4) * 4 + (zlo + j % 4) % 4))
        return carry

    lax.fori_loop(1, 16, greet_col, 0)
    greet(other)
    greet(at_x(x + 1))
    greet(at_x(x + 3))

    greet(at_z(z + 1))
    greet(at_z(z + 7))
    pl.semaphore_wait(barrier, 20)

    def a2a(j):
        dest = ((y + j % 4) % 4) * 4 + apart(j // 4)
        return copy_to((row, dest), eig.at[dest], v_buf.at[0, j], a_send.at[j], a_recv.at[j])

    def apart(k):
        low, high = (zlo + k) % 2, (zlo // 2 + k // 2) % 2
        return high * 2 + low

    def send_a2a(i, carry):
        a2a(i + 1).start()
        return carry

    lax.fori_loop(0, 15, send_a2a, 0)
    for i in range(8):
        give_s(i).start()
    def forward(j):
        return copy_to(other, v_buf.at[0, j], v_buf.at[1, j], f_send.at[j], f_recv.at[j])

    load_v.wait()
    forward(0).start()
    for i in range(8):
        load_s(i).wait()
        s_buf[0, 128 * i:128 * i + 128] = s_raw[0, i].T
    for i in range(8):
        give_s(i).wait_recv()
        s_buf[1, 128 * i:128 * i + 128] = s_raw[1, i].T

    def multiply(i):
        zs = apart(i // 2)
        got = None
        for q in range(2):
            two = jnp.concatenate([v_buf[q, 2 * i], v_buf[q, 2 * i + 1]], axis=1)
            one = jnp.dot(s_buf[q], two, preferred_element_type=jnp.float32)
            got = one if got is None else got + one
        for h in range(2):
            ys = (y + 4 - (2 * i + h) % 4) % 4
            for xi in range(4):
                for zh in range(2):
                    at = (xi * 2 + zh) * 128
                    part[xi, ys, zh, zs] = got[at:at + 128, h * 128:h * 128 + 128]

    def take(j):
        a2a(j).wait_recv()
        forward(j).start()

    where = (row, col, x, y, zhi, zlo, core), (at_x, at_y, at_z, other)
    groups, first, per = [], 0, len(rest) // len(GROUPS)
    for g, sizes in enumerate(GROUPS):
        own = rest[g * per:(g + 1) * per]
        groups.append(Group(where, part, ar, ac, first, sizes, own[:29], own[29:]))
        first += sum(sizes)
    def step(i, carry):
        take(2 * i)
        take(2 * i + 1)
        forward(2 * i - 2).wait_recv()
        forward(2 * i - 1).wait_recv()
        multiply(i - 1)
        return carry

    def drain(i):
        forward(2 * i).wait_recv()
        forward(2 * i + 1).wait_recv()
        multiply(i)

    r_out[...] = jnp.zeros_like(r_out)

    def pair(i):
        a = jnp.concatenate([ar[2 * i], ar[2 * i + 1]], axis=1)
        b = jnp.concatenate([ac[2 * i], ac[2 * i + 1]], axis=1)
        b_hi = b.astype(jnp.bfloat16)
        b_lo = (b - b_hi.astype(jnp.float32)).astype(jnp.bfloat16)
        both = jnp.concatenate([b_hi, b_lo], axis=0)
        p = poles[:, pl.ds(pl.multiple_of(256 * i, 256), 256)]
        his, los = [], []
        for e in range(8):
            scaled = a * p[e:e + 1]
            hi = scaled.astype(jnp.bfloat16)
            his.append(hi)
            los.append((scaled - hi.astype(jnp.float32)).astype(jnp.bfloat16))
        hi = jnp.concatenate(his, axis=0)
        lo = jnp.concatenate(los, axis=0)
        contract = (((1,), (1,)), ((), ()))
        one = lax.dot_general(hi, both, contract, preferred_element_type=jnp.float32)
        two = lax.dot_general(lo, b_hi, contract, preferred_element_type=jnp.float32)
        r_out[...] += (one[:, :128] + (one[:, 128:] + two)).reshape(8, 128, 128)

    a, = groups
    take(1)
    lax.fori_loop(1, 4, step, 0)
    drain(3)
    a.x1n.start()
    a.y1n.start()
    a.x1n.middle()
    a.y1n.middle()
    take(8)
    take(9)
    step(5, 0)
    drain(5)
    a.x1m.start()
    a.y1m.start()
    a.x1n.finish()
    a.x2n.start()
    take(12)
    take(13)
    a.y1n.finish()
    a.y2n.start()
    step(7, 0)
    a.x1m.middle()
    a.y1m.middle()
    drain(7)
    a.z1.start()
    a.x1f.start()
    a.y1f.start()
    a.z1.step(2)
    a.z1.step(3)
    a.x2n.middle()
    a.y2n.middle()
    a.z1.step(4)
    a.x1f.middle()
    a.y1f.middle()
    a.z1.step(5)
    a.x1m.finish()
    a.x2m.start()
    a.y1m.finish()
    a.y2m.start()
    a.z1.step(6)
    a.x1f.finish()
    a.x2f.start()
    a.y1f.finish()
    a.y2f.start()
    a.x2n.finish()
    a.y2n.finish()
    a.z1.finish()
    a.z2.start()
    a.x2m.middle()
    a.y2m.middle()
    a.start_last_z(1, 4, 5)
    a.x2f.middle()
    a.y2f.middle()
    a.x2m.finish()
    a.y2m.finish()
    a.start_last_z(2, 6)
    a.z2.middle()
    a.x2f.finish()
    a.y2f.finish()
    a.start_last_z(3, 7)
    a.z2.finish()
    a.start_last_y()
    a.finish_sums()
    a.start_gather()
    amp_out[...] = ar[col]
    a.middle_gather()
    a.pass_on(0)
    for k in range(4):
        if k < 3:
            a.pass_on(k + 1)
        a.arrive(k)
        for q in range(2):
            pair((y + 4 - k) % 4 * 2 + q)

    def close_a2a(j, carry):
        a2a(j).wait_send()
        return carry

    lax.fori_loop(1, 16, close_a2a, 0)

    def close_forward(j, carry):
        forward(j).wait_send()
        return carry

    lax.fori_loop(0, 16, close_forward, 0)
    for i in range(8):
        give_s(i).wait_send()
    for g in groups:
        g.close_sums()
        g.close_gather()


def local(surface, eigvec, eig_energy, energies):
    width = surface.shape[1]
    f32, bf16 = jnp.float32, jnp.bfloat16
    dma = pltpu.SemaphoreType.DMA
    vmem = pl.BlockSpec(memory_space=pltpu.VMEM)
    return pl.pallas_call(
        kernel,
        out_shape=(jax.ShapeDtypeStruct((128, 128), f32), jax.ShapeDtypeStruct((8, 128, 128), f32)),
        in_specs=[pl.BlockSpec(memory_space=pl.ANY)] * 2 + [vmem],
        out_specs=(vmem, vmem),
        scratch_shapes=[
            pltpu.VMEM((2, 8, width, 128), bf16),
            pltpu.VMEM((2, 1024, width), bf16),
            pltpu.VMEM((2, 16, width, 128), bf16),
            pltpu.VMEM((4, 4, 2, 4, 128, 128), f32),
            pltpu.VMEM((16, 128, 128), f32),
            pltpu.VMEM((16, 128, 128), f32),
            dma((9,)), dma((8,)), dma((8,)), dma((16,)), dma((16,)), dma((16,)), dma((16,)),
        ] + [item for sizes in GROUPS for item in group_buffers(sizes) + group_sems()],
        compiler_params=pltpu.CompilerParams(
            collective_id=0, has_side_effects=True, vmem_limit_bytes=52 * 1024 * 1024
        ),
    )(
        surface.T,
        eigvec.reshape(16, width, 128),
        (1.0 / math.sqrt(2048.0)) / (eig_energy[None, :] - energies[:, None]),
    )


def solution(mesh):
    in_specs = (P(None, ("row", "col")), P("row", "col"), P(), P())
    out_specs = (P("row", "col"), P(None, "row", "col"))
    return jax.shard_map(local, mesh=mesh, in_specs=in_specs, out_specs=out_specs, check_vma=False)
```

```python
import functools
import math

import jax
import jax.numpy as jnp
from jax import lax
from jax.experimental import pallas as pl
from jax.experimental.pallas import tpu as pltpu
from jax.sharding import PartitionSpec as P

MESH = pl.DeviceIdType.MESH
GROUPS = ((56, 48, 24),)


def copy_to(device, src, dst, send, recv):
    return pltpu.make_async_remote_copy(
        src_ref=src, dst_ref=dst, send_sem=send, recv_sem=recv, device_id=device, device_id_type=MESH
    )


def add_into(dst, *srcs):
    shape = dst.shape
    if len(shape) == 2:
        total = dst[...]
        for s in srcs:
            total = total + s[...]
        dst[...] = total
        return
    lead = shape[:-2]
    count = math.prod(lead)

    def body(i, carry):
        at = (i,) if len(lead) == 1 else (i // lead[1], i % lead[1])
        total = dst[at]
        for s in srcs:
            total = total + s[at]
        dst[at] = total
        return carry

    lax.fori_loop(0, count, body, 0)


class Ring4:
    def __init__(self, at, plus, minus, chunk, far, near, send, recv):
        self.at, self.chunk, self.near = at, chunk, near
        up, down, across = (at + 1) % 4, (at + 3) % 4, (at + 2) % 4
        self.up, self.down, self.far = up, down, far
        c = functools.partial
        self.p1 = copy_to(plus, chunk(across, 0), far.at[0], send.at[0], recv.at[0])
        self.m1 = copy_to(minus, chunk(across, 1), far.at[1], send.at[1], recv.at[1])
        self.p2 = copy_to(plus, chunk(up, 1), near.at[0, 1], send.at[2], recv.at[2])
        self.m2 = copy_to(minus, chunk(down, 0), near.at[1, 0], send.at[3], recv.at[3])
        self.p3 = copy_to(plus, chunk(up, 0), near.at[0, 0], send.at[4], recv.at[4])
        self.m3 = copy_to(minus, chunk(down, 1), near.at[1, 1], send.at[5], recv.at[5])

    def start(self):
        for c in (self.p1, self.m1, self.p2, self.m2):
            c.start()

    def middle(self):
        self.p1.wait_recv()
        add_into(self.chunk(self.up, 0), self.far.at[0])
        self.p3.start()
        self.m1.wait_recv()
        add_into(self.chunk(self.down, 1), self.far.at[1])
        self.m3.start()

    def finish(self):
        for c in (self.p2, self.m2, self.p3, self.m3):
            c.wait_recv()
        for h in range(2):
            add_into(self.chunk(self.at, h), self.near.at[0, h], self.near.at[1, h])

    def close(self):
        for c in (self.p1, self.m1, self.p2, self.m2, self.p3, self.m3):
            c.wait_send()


class Ring8:
    def __init__(self, at, plus, minus, chunk, slots, send, recv):
        self.at, self.chunk, self.slots = at, chunk, slots
        self.copies, self.held = [], []
        for s in range(7):
            k = 4 - (s + 1) // 2
            h = 0 if s % 2 == 0 else 1
            pair, held = [], []
            for way, device in ((0, plus), (1, minus)):
                i = (at + k) % 8 if way == 0 else (at + 8 - k) % 8
                half = h if way == 0 else 1 - h
                view = chunk(i, half)
                held.append(view)
                pair.append(copy_to(device, view, slots.at[way, s], send.at[way, s], recv.at[way, s]))
            self.copies.append(pair)
            self.held.append(held)

    def start(self):
        for s in range(2):
            for c in self.copies[s]:
                c.start()

    def step(self, s):
        for way in range(2):
            self.copies[s - 2][way].wait_recv()
            add_into(self.held[s][way], self.slots.at[way, s - 2])
            self.copies[s][way].start()

    def finish(self):
        for s in (5, 6):
            for way in range(2):
                self.copies[s][way].wait_recv()
        add_into(self.chunk(self.at, 0), self.slots.at[0, 6], self.slots.at[1, 5])
        add_into(self.chunk(self.at, 1), self.slots.at[0, 5], self.slots.at[1, 6])

    def close(self):
        for pair in self.copies:
            for c in pair:
                c.wait_send()


class Group:
    def __init__(self, where, part, ar, ac, first, sizes, buf, sem):
        (row, col, x, y, zhi, zlo, core), (at_x, at_y, at_z, other) = where
        z = zhi * 4 + zlo
        nx, ny, nz = sizes
        xr, yr, zr = pl.ds(first, nx), pl.ds(first + nx, ny), pl.ds(first + nx + ny, nz)
        self.xy, self.zr, self.all = pl.ds(first, nx + ny), zr, pl.ds(first, nx + ny + nz)
        self.where, self.part, self.ar, self.ac, self.sem, self.buf = where, part, ar, ac, sem, buf
        xp, xm, yp, ym, zp, zm = at_x(x + 1), at_x(x + 3), at_y(y + 1), at_y(y + 3), at_z(z + 1), at_z(z + 7)
        quarter = lambda h: pl.ds(2 * h, 2)
        ring = lambda k, i, plus, minus, chunk: Ring4(i, plus, minus, chunk, buf[2 * k], buf[2 * k + 1], sem[k].at[0], sem[k].at[1])
        near = pl.ds(zlo // 2 * 2, 2)
        mid, far = (zlo + 2) % 4, (zlo // 2 + 1) % 2 * 2 + (zlo + 1) % 2
        self.x1n = ring(0, x, xp, xm, lambda i, h: part.at[i, :, h, near, xr])
        self.x1m = ring(1, x, xp, xm, lambda i, h: part.at[i, :, h, mid, xr])
        self.x1f = ring(2, x, xp, xm, lambda i, h: part.at[i, :, h, far, xr])
        self.y1n = ring(3, y, yp, ym, lambda i, h: part.at[:, i, h, near, yr])
        self.y1m = ring(4, y, yp, ym, lambda i, h: part.at[:, i, h, mid, yr])
        self.y1f = ring(5, y, yp, ym, lambda i, h: part.at[:, i, h, far, yr])
        self.x2n = ring(6, y, yp, ym, lambda i, h: part.at[x, i, h, near, xr])
        self.x2m = ring(7, y, yp, ym, lambda i, h: part.at[x, i, h, mid, xr])
        self.x2f = ring(8, y, yp, ym, lambda i, h: part.at[x, i, h, far, xr])
        self.y2n = ring(9, x, xp, xm, lambda i, h: part.at[i, y, h, near, yr])
        self.y2m = ring(10, x, xp, xm, lambda i, h: part.at[i, y, h, mid, yr])
        self.y2f = ring(11, x, xp, xm, lambda i, h: part.at[i, y, h, far, yr])
        self.z2 = ring(12, x, xp, xm, lambda i, h: part.at[i, quarter(h), zhi, zlo, zr])
        self.rings = (
            self.x1n, self.x1m, self.x1f, self.y1n, self.y1m, self.y1f,
            self.x2n, self.x2m, self.x2f, self.y2n, self.y2m, self.y2f, self.z2,
        )
        self.z1 = Ring8(z, zp, zm, lambda i, h: part.at[quarter(h), :, i // 4, i % 4, zr], buf[26], sem[13].at[0], sem[13].at[1])
        self.last_z = []
        for k in range(1, 8):
            high, low = (zhi + k // 4) % 2, ((zlo // 2 + k // 2) % 2) * 2 + (zlo + k) % 2
            self.last_z.append(copy_to(
                (x * 4 + high * 2 + core, y * 4 + low), part.at[x, y, high, low, self.xy], buf[27].at[k - 1],
                sem[14].at[0, k], sem[14].at[1, k],
            ))
        self.last_y = [
            copy_to(at_y(y + k), part.at[x, (y + k) % 4, zhi, zlo, zr], buf[28].at[k - 1], sem[15].at[0, k], sem[15].at[1, k])
            for k in range(1, 4)
        ]

    def start_last_z(self, *ks):
        for k in ks:
            self.last_z[k - 1].start()

    def start_last_y(self):
        for c in self.last_y:
            c.start()

    def finish_sums(self):
        (row, col, x, y, zhi, zlo, core), _ = self.where
        for rows, copies, slots in ((self.zr, self.last_y, self.buf[28]), (self.xy, self.last_z, self.buf[27])):
            total = self.part[x, y, zhi, zlo, rows]
            for k, c in enumerate(copies):
                c.wait_recv()
                total = total + slots[k]
            self.ar[col, rows] = total

    def near(self, there, device, k):
        view = self.ar.at[there, self.all]
        return copy_to(device, view, view, self.sem[16].at[0, k], self.sem[16].at[1, k])

    def near_send(self, k):
        (row, col, x, y, zhi, zlo, core), _ = self.where
        return self.near(col, (row, y * 4 + (zlo + k) % 4), k)

    def near_recv(self, k):
        (row, col, x, y, zhi, zlo, core), _ = self.where
        there = y * 4 + (zlo + 4 - k) % 4
        return self.near(there, (row, there), k)

    def along_y(self, there, j, k):
        (row, col, x, y, zhi, zlo, core), (at_x, at_y, at_z, other) = self.where
        view = self.ar.at[there, self.all]
        return copy_to(at_y(y + k), view, view, self.sem[17].at[0, j, k], self.sem[17].at[1, j, k])

    def along_y_send(self, j, k):
        (row, col, x, y, zhi, zlo, core), _ = self.where
        return self.along_y(y * 4 + (zlo + 4 - j) % 4, j, k)

    def along_y_recv(self, j, k):
        (row, col, x, y, zhi, zlo, core), _ = self.where
        return self.along_y(((y + 4 - k) % 4) * 4 + (zlo + 4 - j) % 4, j, k)

    def across(self, i):
        (row, col, x, y, zhi, zlo, core), _ = self.where
        device = (((x + i // 2) % 4) * 4 + ((zhi + i % 2) % 2) * 2 + zlo % 2, row)
        return copy_to(device, self.ar.at[col, self.all], self.ac.at[col, self.all], self.sem[18].at[i], self.sem[19].at[col // 2])

    def stay(self):
        (row, col, x, y, zhi, zlo, core), _ = self.where
        return pltpu.make_async_copy(self.ar.at[col, self.all], self.ac.at[col, self.all], self.sem[19].at[col // 2])

    def hand(self, s):
        (row, col, x, y, zhi, zlo, core), (at_x, at_y, at_z, other) = self.where
        view = self.ac.at[s, self.all]
        return copy_to(other, view, view, self.sem[20].at[0, s], self.sem[20].at[1, s])

    def start_gather(self):
        (row, col, x, y, zhi, zlo, core), _ = self.where
        for k in range(1, 4):
            self.near_send(k).start()
        for i in (5, 4, 3, 7, 1):
            self.across(i).start()
        for k in (2, 1, 3):
            self.along_y_send(0, k).start()
        for i in (2, 6):
            self.across(i).start()

        @pl.when(row == col)
        def _():
            self.stay().start()

        @pl.when(row != col)
        def _():
            self.across(0).start()

    def middle_gather(self):
        for j in range(1, 4):
            self.near_recv(j).wait_recv()
            for k in (2, 1, 3):
                self.along_y_send(j, k).start()

    def pass_on(self, k):
        (row, col, x, y, zhi, zlo, core), (at_x, at_y, at_z, other) = self.where
        for q in range(2):
            s = (y + 4 - k) % 4 * 4 + 2 * q + core
            view = self.ac.at[s, self.all]
            copy_to(other, view, view, self.sem[18].at[0], self.sem[19].at[s // 2]).wait_recv()
            self.hand(s).start()

    def arrive(self, k):
        (row, col, x, y, zhi, zlo, core), _ = self.where
        for j in range(4):
            if k > 0:
                self.along_y_recv(j, k).wait_recv()
        for q in range(2):
            self.hand((y + 4 - k) % 4 * 4 + 2 * q + 1 - core).wait_recv()

    def close_sums(self):
        for ring in self.rings + (self.z1,):
            ring.close()
        for c in self.last_z + self.last_y:
            c.wait_send()

    def close_gather(self):
        (row, col, x, y, zhi, zlo, core), _ = self.where
        for k in range(1, 4):
            self.near_send(k).wait_send()
            for j in range(4):
                self.along_y_send(j, k).wait_send()

        @pl.when(row != col)
        def _():
            self.across(0).wait_send()

        for i in range(1, 8):
            self.across(i).wait_send()

        def body(j, carry):
            self.hand(2 * j + core).wait_send()
            return carry

        lax.fori_loop(0, 8, body, 0)


def group_buffers(sizes):
    nx, ny, nz = sizes
    one = lambda *lead: [(2,) + lead, (2, 2) + lead]
    shapes = one(4, 2, nx) + one(4, nx) * 2 + one(4, 2, ny) + one(4, ny) * 2
    shapes += one(2, nx) + one(nx) * 2 + one(2, ny) + one(ny) * 2 + one(2, nz)
    shapes += [(2, 7, 2, 4, nz), (7, nx + ny), (3, nz)]
    return [pltpu.VMEM(s + (128,), jnp.float32) for s in shapes]


def group_sems():
    shapes = [(2, 6)] * 13 + [(2, 2, 7), (2, 8), (2, 4), (2, 4), (2, 4, 4), (8,), (8,), (2, 16)]
    return [pltpu.SemaphoreType.DMA(s) for s in shapes]


def kernel(
    surf, eig, poles, amp_out, r_out, s_raw, s_buf, v_buf, part, ar, ac,
    loc_sem, s_send, s_recv, a_send, a_recv, f_send, f_recv, *rest,
):
    row, col = lax.axis_index("row"), lax.axis_index("col")
    x, zhi, core = row // 4, (row // 2) % 2, row % 2
    y, zlo = col // 4, col % 4
    z = zhi * 4 + zlo
    other = (row + 1 - 2 * core, col)

    def at_x(i):
        return ((i % 4) * 4 + zhi * 2 + core, col)

    def at_y(i):
        return (row, (i % 4) * 4 + zlo)

    def at_z(i):
        i = i % 8
        return (x * 4 + (i // 4) * 2 + core, y * 4 + i % 4)

    def load_s(i):
        return pltpu.make_async_copy(surf.at[:, columns(2 * i + core)], s_raw.at[0, i], loc_sem.at[i])

    def give_s(i):
        return copy_to(other, surf.at[:, columns(2 * i + 1 - core)], s_raw.at[1, i], s_send.at[i], s_recv.at[i])

    def columns(i):
        return pl.ds(pl.multiple_of(128 * i, 128), 128)

    for i in range(8):
        load_s(i).start()
    load_v = pltpu.make_async_copy(eig.at[col], v_buf.at[0, 0], loc_sem.at[8])
    load_v.start()

    barrier = pltpu.get_barrier_semaphore()

    def greet(device):
        pl.semaphore_signal(barrier, inc=1, device_id=device, device_id_type=MESH)

    def greet_col(j, carry):
        greet((row, ((y + j // 4) % 4) * 4 + (zlo + j % 4) % 4))
        return carry

    lax.fori_loop(1, 16, greet_col, 0)
    greet(other)
    greet(at_x(x + 1))
    greet(at_x(x + 3))

    greet(at_z(z + 1))
    greet(at_z(z + 7))
    pl.semaphore_wait(barrier, 20)

    def a2a(j):
        dest = ((y + j % 4) % 4) * 4 + apart(j // 4)
        return copy_to((row, dest), eig.at[dest], v_buf.at[0, j], a_send.at[j], a_recv.at[j])

    def apart(k):
        low, high = (zlo + k) % 2, (zlo // 2 + k // 2) % 2
        return high * 2 + low

    def send_a2a(i, carry):
        a2a(i + 1).start()
        return carry

    lax.fori_loop(0, 15, send_a2a, 0)
    for i in range(8):
        give_s(i).start()
    def forward(j):
        return copy_to(other, v_buf.at[0, j], v_buf.at[1, j], f_send.at[j], f_recv.at[j])

    load_v.wait()
    forward(0).start()
    for i in range(8):
        load_s(i).wait()
        s_buf[0, 128 * i:128 * i + 128] = s_raw[0, i].T
    for i in range(8):
        give_s(i).wait_recv()
        s_buf[1, 128 * i:128 * i + 128] = s_raw[1, i].T

    def multiply(i):
        zs = apart(i // 2)
        got = None
        for q in range(2):
            two = jnp.concatenate([v_buf[q, 2 * i], v_buf[q, 2 * i + 1]], axis=1)
            one = jnp.dot(s_buf[q], two, preferred_element_type=jnp.float32)
            got = one if got is None else got + one
        for h in range(2):
            ys = (y + 4 - (2 * i + h) % 4) % 4
            for xi in range(4):
                for zh in range(2):
                    at = (xi * 2 + zh) * 128
                    part[xi, ys, zh, zs] = got[at:at + 128, h * 128:h * 128 + 128]

    def take(j):
        a2a(j).wait_recv()
        forward(j).start()

    where = (row, col, x, y, zhi, zlo, core), (at_x, at_y, at_z, other)
    groups, first, per = [], 0, len(rest) // len(GROUPS)
    for g, sizes in enumerate(GROUPS):
        own = rest[g * per:(g + 1) * per]
        groups.append(Group(where, part, ar, ac, first, sizes, own[:29], own[29:]))
        first += sum(sizes)
    def step(i, carry):
        take(2 * i)
        take(2 * i + 1)
        forward(2 * i - 2).wait_recv()
        forward(2 * i - 1).wait_recv()
        multiply(i - 1)
        return carry

    def drain(i):
        forward(2 * i).wait_recv()
        forward(2 * i + 1).wait_recv()
        multiply(i)

    r_out[...] = jnp.zeros_like(r_out)

    def pair(i):
        a = jnp.concatenate([ar[2 * i], ar[2 * i + 1]], axis=1)
        b = jnp.concatenate([ac[2 * i], ac[2 * i + 1]], axis=1)
        b_hi = b.astype(jnp.bfloat16)
        b_lo = (b - b_hi.astype(jnp.float32)).astype(jnp.bfloat16)
        both = jnp.concatenate([b_hi, b_lo], axis=0)
        p = poles[:, pl.ds(pl.multiple_of(256 * i, 256), 256)]
        his, los = [], []
        for e in range(8):
            scaled = a * p[e:e + 1]
            hi = scaled.astype(jnp.bfloat16)
            his.append(hi)
            los.append((scaled - hi.astype(jnp.float32)).astype(jnp.bfloat16))
        hi = jnp.concatenate(his, axis=0)
        lo = jnp.concatenate(los, axis=0)
        contract = (((1,), (1,)), ((), ()))
        one = lax.dot_general(hi, both, contract, preferred_element_type=jnp.float32)
        two = lax.dot_general(lo, b_hi, contract, preferred_element_type=jnp.float32)
        r_out[...] += (one[:, :128] + (one[:, 128:] + two)).reshape(8, 128, 128)

    a, = groups
    take(1)
    lax.fori_loop(1, 4, step, 0)
    drain(3)
    a.x1n.start()
    a.y1n.start()
    a.x1n.middle()
    a.y1n.middle()
    take(8)
    take(9)
    step(5, 0)
    drain(5)
    a.x1m.start()
    a.y1m.start()
    a.x1n.finish()
    a.x2n.start()
    take(12)
    take(13)
    a.y1n.finish()
    a.y2n.start()
    step(7, 0)
    a.x1m.middle()
    a.y1m.middle()
    drain(7)
    a.z1.start()
    a.x1f.start()
    a.y1f.start()
    a.z1.step(2)
    a.z1.step(3)
    a.x2n.middle()
    a.y2n.middle()
    a.z1.step(4)
    a.x1f.middle()
    a.y1f.middle()
    a.z1.step(5)
    a.x1m.finish()
    a.x2m.start()
    a.y1m.finish()
    a.y2m.start()
    a.z1.step(6)
    a.x1f.finish()
    a.x2f.start()
    a.y1f.finish()
    a.y2f.start()
    a.x2n.finish()
    a.y2n.finish()
    a.z1.finish()
    a.z2.start()
    a.x2m.middle()
    a.y2m.middle()
    a.start_last_z(1, 4, 5)
    a.x2f.middle()
    a.y2f.middle()
    a.x2m.finish()
    a.y2m.finish()
    a.start_last_z(2, 6)
    a.z2.middle()
    a.x2f.finish()
    a.y2f.finish()
    a.start_last_z(3, 7)
    a.z2.finish()
    a.start_last_y()
    a.finish_sums()
    a.start_gather()
    amp_out[...] = ar[col]
    a.middle_gather()
    a.pass_on(0)
    for k in range(4):
        if k < 3:
            a.pass_on(k + 1)
        a.arrive(k)
        for q in range(2):
            pair((y + 4 - k) % 4 * 2 + q)

    def close_a2a(j, carry):
        a2a(j).wait_send()
        return carry

    lax.fori_loop(1, 16, close_a2a, 0)

    def close_forward(j, carry):
        forward(j).wait_send()
        return carry

    lax.fori_loop(0, 16, close_forward, 0)
    for i in range(8):
        give_s(i).wait_send()
    for g in groups:
        g.close_sums()
        g.close_gather()


def local(surface, eigvec, eig_energy, energies):
    width = surface.shape[1]
    f32, bf16 = jnp.float32, jnp.bfloat16
    dma = pltpu.SemaphoreType.DMA
    vmem = pl.BlockSpec(memory_space=pltpu.VMEM)
    return pl.pallas_call(
        kernel,
        out_shape=(jax.ShapeDtypeStruct((128, 128), f32), jax.ShapeDtypeStruct((8, 128, 128), f32)),
        in_specs=[pl.BlockSpec(memory_space=pl.ANY)] * 2 + [vmem],
        out_specs=(vmem, vmem),
        scratch_shapes=[
            pltpu.VMEM((2, 8, width, 128), bf16),
            pltpu.VMEM((2, 1024, width), bf16),
            pltpu.VMEM((2, 16, width, 128), bf16),
            pltpu.VMEM((4, 4, 2, 4, 128, 128), f32),
            pltpu.VMEM((16, 128, 128), f32),
            pltpu.VMEM((16, 128, 128), f32),
            dma((9,)), dma((8,)), dma((8,)), dma((16,)), dma((16,)), dma((16,)), dma((16,)),
        ] + [item for sizes in GROUPS for item in group_buffers(sizes) + group_sems()],
        compiler_params=pltpu.CompilerParams(
            collective_id=0, has_side_effects=True, vmem_limit_bytes=52 * 1024 * 1024
        ),
    )(
        surface.T,
        eigvec.reshape(16, width, 128),
        (1.0 / math.sqrt(2048.0)) / (eig_energy[None, :] - energies[:, None]),
    )


def solution(mesh):
    in_specs = (P(None, ("row", "col")), P("row", "col"), P(), P())
    out_specs = (P("row", "col"), P(None, "row", "col"))
    return jax.shard_map(local, mesh=mesh, in_specs=in_specs, out_specs=out_specs, check_vma=False)
```
